1024 devices in a mesh: gx: 128 (over y, z), gy: 8 (over x, core).
Axes of the slice: x: 4, y: 4, z: 32, core: 2. Of those that a mesh axis runs over, the one named last changes fastest.
Arguments:
- density: float32 [512, 256, 256], P('gx', 'gy'), may hold values from -6 to 6
- field: float32 [512, 256, 256], P('gx', 'gy'), may hold values from -4 to 4
Outputs:
- updated: float32 [512, 256, 256], P('gx', 'gy')
The draws below stay inside these ranges and needn't reach their ends.
All inputs are finite; a program needn't handle non-finite values.
Results may differ from the reference program's by a relative error of at most 0.00002.
Values sent between devices are 32-bit elements; how exact they have to be, the bound alone decides.
No kernel may reach another device: no remote copies, remote signals or barrier semaphores. Data moves between devices by JAX's collectives and lax.ppermute only.
A program may use at most 64 MiB of HBM per device.

```python
import jax
import jax.numpy as jnp

CZ = 256
PRE_SWEEPS = 2
POST_SWEEPS = 2
COARSE_SWEEPS = 6
NX = 512
NY = 256


def level_of(key, shape, cuts, smallest, largest):
    factor_of = 1.0
    for dim, parts in cuts:
        heights = jax.random.uniform(jax.random.fold_in(jax.random.fold_in(key, 6), dim), (parts,), jnp.float32, smallest / len(cuts), largest / len(cuts))
        factor_of = factor_of * jnp.repeat(jnp.exp(heights), shape[dim] // parts).reshape((-1,) + (1,) * (len(shape) - 1 - dim))
    return factor_of


def scatter_about(stream_key, extent, deviation, limit, split=(), kind=jnp.bfloat16):
    level = level_of(stream_key, extent, split, -0.22, 0.18) if split else 1.0
    array = jax.random.normal(stream_key, extent, jnp.float32) * deviation * level
    return jnp.minimum(jnp.maximum(array, -limit), limit).astype(kind)


def setup_inputs(seed: int = 0) -> dict:
    key_list = jax.random.split(jax.random.key(seed), 3)
    return {
        "density": scatter_about(key_list[0], (NX, NY, CZ), 1.0, 6.0, ((0, 128), (1, 8)), jnp.float32),
        "field": scatter_about(key_list[1], (NX, NY, CZ), 0.7, 4.0, ((0, 128), (1, 8)), jnp.float32),
    }


mass_term = 0.02
damping = 0.8


def neighbours(values):
    total = jnp.roll(values, -1, 0) + jnp.roll(values, 1, 0)
    total = total + jnp.roll(values, -1, 1) + jnp.roll(values, 1, 1)
    total = total + jnp.roll(values, -1, 2) + jnp.roll(values, 1, 2)
    return total


def operator(values, around, inv_step):
    return inv_step * (around - 6.0 * values) - mass_term * (values + values * values * values / 3.0)


def jacobi(values, source, around, inv_step):
    misfit = operator(values, around, inv_step) - source
    slope = -6.0 * inv_step - mass_term * (1.0 + values * values)
    return values - damping * misfit / slope


def restrict(values):
    first, second, third = values.shape
    return values.reshape(first // 2, 2, second // 2, 2, third // 2, 2).mean(axis=(1, 3, 5))


def spread(center, minus, plus, axis):
    even = 0.75 * center + 0.25 * minus
    odd = 0.75 * center + 0.25 * plus
    both = jnp.stack([even, odd], axis=axis + 1)
    shape = list(center.shape)
    shape[axis] = shape[axis] * 2
    return both.reshape(shape)


def prolong(values):
    for axis in range(3):
        values = spread(values, jnp.roll(values, 1, axis), jnp.roll(values, -1, axis), axis)
    return values


def reference(density, field):
    current = field
    for sweep in range(PRE_SWEEPS):
        current = jacobi(current, density, neighbours(current), 1.0)
    defect = density - operator(current, neighbours(current), 1.0)
    start = restrict(current)
    coarse_source = operator(start, neighbours(start), 0.25) + restrict(defect)
    coarse = start
    for sweep in range(COARSE_SWEEPS):
        coarse = jacobi(coarse, coarse_source, neighbours(coarse), 0.25)
    current = current + prolong(coarse - start)
    for sweep in range(POST_SWEEPS):
        current = jacobi(current, density, neighbours(current), 1.0)
    return current
```

```python
import jax
import jax.numpy as jnp
from jax import lax
from jax.experimental import pallas as pl
from jax.experimental.pallas import tpu as pltpu
from jax.sharding import PartitionSpec as P

mass = 0.02
damping = 0.8


def jacobi(v, below, above, source, inv_step):
    around = below + above
    around = around + pltpu.roll(v, 1, 0) + pltpu.roll(v, v.shape[0] - 1, 0)
    around = around + pltpu.roll(v, 1, 1) + pltpu.roll(v, v.shape[1] - 1, 1)
    square = v * v
    top = inv_step * around - source - v * ((6.0 * inv_step + mass) + (mass / 3.0) * square)
    return v + top / ((6.0 * inv_step + mass) / damping + (mass / damping) * square)


def operator(v, below, above, inv_step):
    around = below + above
    around = around + pltpu.roll(v, 1, 0) + pltpu.roll(v, v.shape[0] - 1, 0)
    around = around + pltpu.roll(v, 1, 1) + pltpu.roll(v, v.shape[1] - 1, 1)
    return inv_step * around - v * ((6.0 * inv_step + mass) + (mass / 3.0) * (v * v))


def exact_dot(values, weights):
    high = values.astype(jnp.bfloat16)
    rest = values - high.astype(jnp.float32)
    middle = rest.astype(jnp.bfloat16)
    low = (rest - middle.astype(jnp.float32)).astype(jnp.bfloat16)
    total = jnp.dot(low, weights, preferred_element_type=jnp.float32)
    total = total + jnp.dot(middle, weights, preferred_element_type=jnp.float32)
    return total + jnp.dot(high, weights, preferred_element_type=jnp.float32)


def fine_kernel(field, density, xlo, xhi, ylo, yhi, clo, chi, smooth, dens, coarse, f, d, s1, pair, rows):
    f[0:4, 8:40] = xlo[0:4]
    f[4:8, 8:40] = field[...]
    f[8:12, 8:40] = xhi[0:4]
    d[0:3, 8:40] = xlo[4:7]
    d[3:7, 8:40] = density[...]
    d[7:10, 8:40] = xhi[4:7]
    for corner, side, at in ((clo, ylo, 4), (chi, yhi, 40)):
        f[0:4, at : at + 4] = corner[0:4]
        f[4:8, at : at + 4] = side[:, 0:4]
        f[8:12, at : at + 4] = corner[7:11]
        d[0:3, at : at + 4] = corner[4:7]
        d[3:7, at : at + 4] = side[:, 4:8]
        d[7:10, at : at + 4] = corner[11:14]
    for i in range(10):
        s1[i] = jacobi(f[i + 1], f[i], f[i + 2], d[i], 1.0)
    for i in range(8):
        smooth[i] = jacobi(s1[i + 1], s1[i], s1[i + 2], d[i + 1], 1.0)
    dens[...] = d[2:8]
    for j in range(2):
        total = smooth[2 * j + 2] + smooth[2 * j + 3]
        pair[j, 0], pair[j, 1] = total[:, 0:128], total[:, 128:256]
        defect = [
            d[i + 3] - operator(smooth[i + 2], smooth[i + 1], smooth[i + 3], 1.0) for i in (2 * j, 2 * j + 1)
        ]
        total = defect[0] + defect[1]
        pair[j + 2, 0], pair[j + 2, 1] = total[:, 0:128], total[:, 128:256]
    for j in range(4):
        for k in range(2):
            total = pair[j, k, pl.ds(8, 16, stride=2)] + pair[j, k, pl.ds(9, 16, stride=2)]
            rows[16 * j : 16 * j + 16, 128 * k : 128 * k + 128] = total
    third = lax.broadcasted_iota(jnp.int32, (256, 128), 0)
    half = lax.broadcasted_iota(jnp.int32, (256, 128), 1)
    weights = jnp.where(third // 2 == half, 0.125, 0.0).astype(jnp.bfloat16)
    coarse[...] = exact_dot(rows[...], weights).reshape(4, 16, 128)


def coarse_kernel(smooth, dens, own, xlo, xhi, flo, fhi, ylo, yhi, clo, chi, glo, ghi, out, a, r, g, c0, c1, wide, corrected, post):
    def place(rows, mine, low, high, far_low, far_high):
        for ref, at in ((a, 0), (r, 1)):
            ref[7:9, rows] = mine[2 * at : 2 * at + 2]
            ref[5:7, rows] = low[2 * at : 2 * at + 2]
            ref[9:11, rows] = high[2 * at : 2 * at + 2]
            ref[0:5, rows] = far_low[5 * at : 5 * at + 5]
            ref[11:16, rows] = far_high[5 * at : 5 * at + 5]

    place(slice(8, 24), own, xlo, xhi, flo, fhi)
    place(slice(0, 8), ylo, clo.at[0:4], clo.at[4:8], glo.at[0:10], glo.at[10:20])
    place(slice(24, 32), yhi, chi.at[0:4], chi.at[4:8], ghi.at[0:10], ghi.at[10:20])
    for i in range(16):
        v = a[i]
        c0[i] = v - r[i] / ((1.5 + mass) / damping + (mass / damping) * (v * v))
    for i in range(1, 15):
        g[i] = operator(a[i], a[i - 1], a[i + 1], 0.25) + r[i]
    now, later = c0, c1
    for sweep in range(1, 6):
        for i in range(sweep, 16 - sweep):
            later[i] = jacobi(now[i], now[i - 1], now[i + 1], g[i], 0.25)
        now, later = later, now
    change = (now[5:11] - a[5:11]).reshape(192, 128)
    half = lax.broadcasted_iota(jnp.int32, (128, 256), 0)
    third = lax.broadcasted_iota(jnp.int32, (128, 256), 1)
    beside = (third // 2 + 2 * (third % 2) - 1 + 128) % 128
    weights = jnp.where(third // 2 == half, 0.75, jnp.where(beside == half, 0.25, 0.0)).astype(jnp.bfloat16)
    spread = exact_dot(change, weights).reshape(6, 32, 256)
    for i in range(6):
        v = spread[i]
        even = 0.75 * v + 0.25 * pltpu.roll(v, 1, 0)
        odd = 0.75 * v + 0.25 * pltpu.roll(v, 31, 0)
        for k in range(2):
            wide[i, k, pl.ds(0, 32, stride=2)] = even[:, 128 * k : 128 * k + 128]
            wide[i, k, pl.ds(1, 32, stride=2)] = odd[:, 128 * k : 128 * k + 128]
    for i in range(8):
        near = i // 2 + 1
        beside_layer = near - 1 if i % 2 == 0 else near + 1
        for k in range(2):
            lanes = slice(128 * k, 128 * k + 128)
            change = 0.75 * wide[near, k, 8:56] + 0.25 * wide[beside_layer, k, 8:56]
            corrected[i, :, lanes] = smooth[i, :, lanes] + change
    for i in range(6):
        post[i] = jacobi(corrected[i + 1], corrected[i], corrected[i + 2], dens[i], 1.0)
    for i in range(4):
        out[i] = jacobi(post[i + 1], post[i], post[i + 2], dens[i + 1], 1.0)[8:40]


def call(kernel, outs, scratch, *args):
    vmem = pl.BlockSpec(memory_space=pltpu.VMEM)
    shapes = [jax.ShapeDtypeStruct(shape, jnp.float32) for shape in outs]
    return pl.pallas_call(
        kernel,
        out_shape=shapes,
        in_specs=[vmem] * len(args),
        out_specs=[vmem] * len(outs),
        scratch_shapes=[pltpu.VMEM(shape, jnp.float32) for shape in scratch],
        compiler_params=pltpu.CompilerParams(vmem_limit_bytes=32 * 1024 * 1024),
    )(*args)


def send(values, axis, step):
    count = lax.axis_size(axis)
    return lax.ppermute(values, axis, [(i, (i + step) % count) for i in range(count)])


def body(density, field):
    xlo = send(jnp.concatenate([field, density[1:4]], 0), "gx", 1)
    xhi = send(jnp.concatenate([field, density[0:3]], 0), "gx", -1)
    ylo = send(jnp.concatenate([field[:, 28:32], density[:, 28:32]], 1), "gy", 1)
    yhi = send(jnp.concatenate([field[:, 0:4], density[:, 0:4]], 1), "gy", -1)
    clo = send(jnp.concatenate([xlo[:, 28:32], xhi[:, 28:32]], 0), "gy", 1)
    chi = send(jnp.concatenate([xlo[:, 0:4], xhi[:, 0:4]], 0), "gy", -1)
    smooth, dens, own = call(
        fine_kernel,
        [(8, 48, 256), (6, 48, 256), (4, 16, 128)],
        [(12, 48, 256), (10, 48, 256), (10, 48, 256), (4, 2, 48, 128), (64, 256)],
        field, density, xlo, xhi, ylo, yhi, clo, chi,
    )
    xlo = send(own, "gx", 1)
    xhi = send(own, "gx", -1)
    ylo = send(own[:, 8:16], "gy", 1)
    yhi = send(own[:, 0:8], "gy", -1)
    flo = send(jnp.concatenate([xlo[1:2], own[0:2], xhi[0:2], xlo[3:4], own[2:4], xhi[2:4]], 0), "gx", 3)
    fhi = send(jnp.concatenate([xlo[0:2], own[0:2], xhi[0:1], xlo[2:4], own[2:4], xhi[2:3]], 0), "gx", -3)
    near = jnp.concatenate([xlo, xhi], 0)
    clo = send(near[:, 8:16], "gy", 1)
    chi = send(near[:, 0:8], "gy", -1)
    far = jnp.concatenate([flo, fhi], 0)
    glo = send(far[:, 8:16], "gy", 1)
    ghi = send(far[:, 0:8], "gy", -1)
    (out,) = call(
        coarse_kernel,
        [(4, 32, 256)],
        [(16, 32, 128), (16, 32, 128), (16, 32, 128), (16, 32, 128), (16, 32, 128), (6, 2, 64, 128), (8, 48, 256), (6, 48, 256)],
        smooth, dens, own, xlo, xhi, flo, fhi, ylo, yhi, clo, chi, glo, ghi,
    )
    return out


def solution(mesh):
    placed = (P("gx", "gy", None), P("gx", "gy", None))
    return jax.shard_map(body, mesh=mesh, in_specs=placed, out_specs=P("gx", "gy", None), check_vma=False)
```

```python
import jax
import jax.numpy as jnp
from jax import lax
from jax.experimental import pallas as pl
from jax.experimental.pallas import tpu as pltpu
from jax.sharding import PartitionSpec as P

mass = 0.02
damping = 0.8


def jacobi(v, below, above, source, inv_step):
    around = below + above
    around = around + pltpu.roll(v, 1, 0) + pltpu.roll(v, v.shape[0] - 1, 0)
    around = around + pltpu.roll(v, 1, 1) + pltpu.roll(v, v.shape[1] - 1, 1)
    square = v * v
    top = inv_step * around - source - v * ((6.0 * inv_step + mass) + (mass / 3.0) * square)
    return v + top / ((6.0 * inv_step + mass) / damping + (mass / damping) * square)


def operator(v, below, above, inv_step):
    around = below + above
    around = around + pltpu.roll(v, 1, 0) + pltpu.roll(v, v.shape[0] - 1, 0)
    around = around + pltpu.roll(v, 1, 1) + pltpu.roll(v, v.shape[1] - 1, 1)
    return inv_step * around - v * ((6.0 * inv_step + mass) + (mass / 3.0) * (v * v))


def exact_dot(values, weights):
    high = values.astype(jnp.bfloat16)
    rest = values - high.astype(jnp.float32)
    middle = rest.astype(jnp.bfloat16)
    low = (rest - middle.astype(jnp.float32)).astype(jnp.bfloat16)
    total = jnp.dot(low, weights, preferred_element_type=jnp.float32)
    total = total + jnp.dot(middle, weights, preferred_element_type=jnp.float32)
    return total + jnp.dot(high, weights, preferred_element_type=jnp.float32)


def fine_kernel(field, density, xlo, xhi, ylo, yhi, clo, chi, smooth, dens, coarse, up, down, f, d, s1, pair, rows):
    f[0:3, 8:40] = xlo[0:3]
    f[3:7, 8:40] = field[...]
    f[7:10, 8:40] = xhi[0:3]
    d[0:2, 8:40] = xlo[3:5]
    d[2:6, 8:40] = density[...]
    d[6:8, 8:40] = xhi[3:5]
    for corner, side, at in ((clo, ylo, 4), (chi, yhi, 40)):
        f[0:3, at : at + 4] = corner[0:3]
        f[3:7, at : at + 4] = side[:, 0:4]
        f[7:10, at : at + 4] = corner[5:8]
        d[0:2, at : at + 4] = corner[3:5]
        d[2:6, at : at + 4] = side[:, 4:8]
        d[6:8, at : at + 4] = corner[8:10]
    for i in range(8):
        s1[i] = jacobi(f[i + 1], f[i], f[i + 2], d[i], 1.0)
    for i in range(6):
        smooth[i] = jacobi(s1[i + 1], s1[i], s1[i + 2], d[i + 1], 1.0)
    dens[...] = d[1:7]
    for j in range(2):
        total = smooth[2 * j + 1] + smooth[2 * j + 2]
        pair[j, 0], pair[j, 1] = total[:, 0:128], total[:, 128:256]
        defect = [
            d[i + 2] - operator(smooth[i + 1], smooth[i], smooth[i + 2], 1.0) for i in (2 * j, 2 * j + 1)
        ]
        total = defect[0] + defect[1]
        pair[j + 2, 0], pair[j + 2, 1] = total[:, 0:128], total[:, 128:256]
    for j in range(4):
        for k in range(2):
            total = pair[j, k, pl.ds(8, 16, stride=2)] + pair[j, k, pl.ds(9, 16, stride=2)]
            rows[16 * j : 16 * j + 16, 128 * k : 128 * k + 128] = total
    third = lax.broadcasted_iota(jnp.int32, (256, 128), 0)
    half = lax.broadcasted_iota(jnp.int32, (256, 128), 1)
    weights = jnp.where(third // 2 == half, 0.125, 0.0).astype(jnp.bfloat16)
    coarse[...] = exact_dot(rows[...], weights).reshape(4, 16, 128)
    for face, layer in ((up, 3), (down, 2)):
        for j in range(4):
            at, lane = 8 + 16 * (j // 2), 128 * (j % 2)
            face[j] = smooth[layer, at : at + 16, lane : lane + 128]


def coarse_kernel(
    smooth, dens, own, flo, fhi, nlo, nhi, yown, yfar, ynear, zown, zfar, znear,
    out, a, r, g, c0, c1, wide, corrected, post,
):
    def place(rows, mine, far_low, far_high, low, high):
        for ref, at in ((a, 0), (r, 1)):
            ref[0:1, rows] = low[at : at + 1]
            ref[1:3, rows] = far_low[2 * at : 2 * at + 2]
            ref[3:5, rows] = high[2 * at + 6 : 2 * at + 8]
            ref[5:7, rows] = low[2 * at + 2 : 2 * at + 4]
            ref[7:9, rows] = mine[2 * at : 2 * at + 2]
            ref[9:11, rows] = high[2 * at + 2 : 2 * at + 4]
            ref[11:13, rows] = low[2 * at + 6 : 2 * at + 8]
            ref[13:15, rows] = far_high[2 * at : 2 * at + 2]
            ref[15:16, rows] = high[at : at + 1]

    place(slice(8, 24), own, flo, fhi, nlo, nhi)
    place(slice(0, 8), yown, yfar.at[0:4], yfar.at[4:8], ynear.at[0:10], ynear.at[10:20])
    place(slice(24, 32), zown, zfar.at[0:4], zfar.at[4:8], znear.at[0:10], znear.at[10:20])
    for i in range(16):
        v = a[i]
        c0[i] = v - r[i] / ((1.5 + mass) / damping + (mass / damping) * (v * v))
    for i in range(1, 15):
        g[i] = operator(a[i], a[i - 1], a[i + 1], 0.25) + r[i]
    now, later = c0, c1
    for sweep in range(1, 6):
        for i in range(sweep, 16 - sweep):
            later[i] = jacobi(now[i], now[i - 1], now[i + 1], g[i], 0.25)
        now, later = later, now
    change = (now[5:11] - a[5:11]).reshape(192, 128)
    half = lax.broadcasted_iota(jnp.int32, (128, 256), 0)
    third = lax.broadcasted_iota(jnp.int32, (128, 256), 1)
    beside = (third // 2 + 2 * (third % 2) - 1 + 128) % 128
    weights = jnp.where(third // 2 == half, 0.75, jnp.where(beside == half, 0.25, 0.0)).astype(jnp.bfloat16)
    spread = exact_dot(change, weights).reshape(6, 32, 256)
    for i in range(6):
        v = spread[i]
        even = 0.75 * v + 0.25 * pltpu.roll(v, 1, 0)
        odd = 0.75 * v + 0.25 * pltpu.roll(v, 31, 0)
        for k in range(2):
            wide[i, k, pl.ds(0, 32, stride=2)] = even[:, 128 * k : 128 * k + 128]
            wide[i, k, pl.ds(1, 32, stride=2)] = odd[:, 128 * k : 128 * k + 128]
    for j in range(4):
        at, lane = 8 + 16 * (j // 2), 128 * (j % 2)
        corrected[0, at : at + 16, lane : lane + 128] = nlo[10 + j]
        corrected[7, at : at + 16, lane : lane + 128] = nhi[10 + j]
    for i in range(8):
        near = i // 2 + 1
        beside_layer = near - 1 if i % 2 == 0 else near + 1
        before = corrected.at[i] if i in (0, 7) else smooth.at[i - 1]
        for k in range(2):
            lanes = slice(128 * k, 128 * k + 128)
            change = 0.75 * wide[near, k, 8:56] + 0.25 * wide[beside_layer, k, 8:56]
            corrected[i, :, lanes] = before[:, lanes] + change
    for i in range(6):
        post[i] = jacobi(corrected[i + 1], corrected[i], corrected[i + 2], dens[i], 1.0)
    for i in range(4):
        out[i] = jacobi(post[i + 1], post[i], post[i + 2], dens[i + 1], 1.0)[8:40]


def call(kernel, outs, scratch, *args):
    vmem = pl.BlockSpec(memory_space=pltpu.VMEM)
    shapes = [jax.ShapeDtypeStruct(shape, jnp.float32) for shape in outs]
    return pl.pallas_call(
        kernel,
        out_shape=shapes,
        in_specs=[vmem] * len(args),
        out_specs=[vmem] * len(outs),
        scratch_shapes=[pltpu.VMEM(shape, jnp.float32) for shape in scratch],
        compiler_params=pltpu.CompilerParams(vmem_limit_bytes=32 * 1024 * 1024),
    )(*args)


def send(values, axis, step):
    count = lax.axis_size(axis)
    return lax.ppermute(values, axis, [(i, (i + step) % count) for i in range(count)])


def rows_from_sides(values):
    height = values.shape[1]
    return send(values[:, height - 8 :], "gy", 1), send(values[:, :8], "gy", -1)


def body(density, field):
    xlo = send(jnp.concatenate([field[1:4], density[2:4]], 0), "gx", 1)
    xhi = send(jnp.concatenate([field[0:3], density[0:2]], 0), "gx", -1)
    ylo = send(jnp.concatenate([field[:, 28:32], density[:, 28:32]], 1), "gy", 1)
    yhi = send(jnp.concatenate([field[:, 0:4], density[:, 0:4]], 1), "gy", -1)
    xlo, xhi, ylo, yhi = lax.optimization_barrier((xlo, xhi, ylo, yhi))
    clo = send(jnp.concatenate([xlo[:, 28:32], xhi[:, 28:32]], 0), "gy", 1)
    chi = send(jnp.concatenate([xlo[:, 0:4], xhi[:, 0:4]], 0), "gy", -1)
    smooth, dens, own, up, down = call(
        fine_kernel,
        [(6, 48, 256), (6, 48, 256), (4, 16, 128), (4, 16, 128), (4, 16, 128)],
        [(10, 48, 256), (8, 48, 256), (8, 48, 256), (4, 2, 48, 128), (64, 256)],
        field, density, xlo, xhi, ylo, yhi, clo, chi,
    )
    flo, fhi = send(own, "gx", 3), send(own, "gx", -3)
    yown, zown = rows_from_sides(own)
    flo, fhi, yown, zown = lax.optimization_barrier((flo, fhi, yown, zown))
    nlo = send(jnp.concatenate([flo[1:2], flo[3:4], own, fhi, up], 0), "gx", 1)
    nhi = send(jnp.concatenate([fhi[0:1], fhi[2:3], own, flo, down], 0), "gx", -1)
    yfar, zfar = rows_from_sides(jnp.concatenate([flo, fhi], 0))
    nlo, nhi, yfar, zfar = lax.optimization_barrier((nlo, nhi, yfar, zfar))
    ynear, znear = rows_from_sides(jnp.concatenate([nlo[0:10], nhi[0:10]], 0))
    (out,) = call(
        coarse_kernel,
        [(4, 32, 256)],
        [(16, 32, 128)] * 5 + [(6, 2, 64, 128), (8, 48, 256), (6, 48, 256)],
        smooth, dens, own, flo, fhi, nlo, nhi, yown, yfar, ynear, zown, zfar, znear,
    )
    return out


def solution(mesh):
    placed = (P("gx", "gy", None), P("gx", "gy", None))
    return jax.shard_map(body, mesh=mesh, in_specs=placed, out_specs=P("gx", "gy", None), check_vma=False)
```

```python
import jax
import jax.numpy as jnp
from jax import lax
from jax.experimental import pallas as pl
from jax.experimental.pallas import tpu as pltpu
from jax.sharding import PartitionSpec as P

mass = 0.02
damping = 0.8


def jacobi(v, below, above, source, inv_step):
    around = below + above
    around = around + pltpu.roll(v, 1, 0) + pltpu.roll(v, v.shape[0] - 1, 0)
    around = around + pltpu.roll(v, 1, 1) + pltpu.roll(v, v.shape[1] - 1, 1)
    square = v * v
    top = inv_step * around - source - v * ((6.0 * inv_step + mass) + (mass / 3.0) * square)
    return v + top / ((6.0 * inv_step + mass) / damping + (mass / damping) * square)


def operator(v, below, above, inv_step):
    around = below + above
    around = around + pltpu.roll(v, 1, 0) + pltpu.roll(v, v.shape[0] - 1, 0)
    around = around + pltpu.roll(v, 1, 1) + pltpu.roll(v, v.shape[1] - 1, 1)
    return inv_step * around - v * ((6.0 * inv_step + mass) + (mass / 3.0) * (v * v))


def exact_dot(values, weights):
    high = values.astype(jnp.bfloat16)
    rest = values - high.astype(jnp.float32)
    middle = rest.astype(jnp.bfloat16)
    low = (rest - middle.astype(jnp.float32)).astype(jnp.bfloat16)
    total = jnp.dot(low, weights, preferred_element_type=jnp.float32)
    total = total + jnp.dot(middle, weights, preferred_element_type=jnp.float32)
    return total + jnp.dot(high, weights, preferred_element_type=jnp.float32)


def fine_kernel(field, density, xlo, xhi, clo, chi, smooth, dens, coarse, up, down, f, d, s1, pair, rows):
    f[0:3, 8:40] = xlo[0:3]
    f[3:7, 8:40] = field[...]
    f[7:10, 8:40] = xhi[0:3]
    d[0:2, 8:40] = xlo[3:5]
    d[2:6, 8:40] = density[...]
    d[6:8, 8:40] = xhi[3:5]
    for side, at in ((clo, 4), (chi, 40)):
        f[0:3, at : at + 4] = side[0:3]
        f[3:7, at : at + 4] = side[10:14]
        f[7:10, at : at + 4] = side[5:8]
        d[0:2, at : at + 4] = side[3:5]
        d[2:6, at : at + 4] = side[14:18]
        d[6:8, at : at + 4] = side[8:10]
    for i in range(8):
        s1[i] = jacobi(f[i + 1], f[i], f[i + 2], d[i], 1.0)
    for i in range(6):
        smooth[i] = jacobi(s1[i + 1], s1[i], s1[i + 2], d[i + 1], 1.0)
    dens[...] = d[1:7]
    for j in range(2):
        total = smooth[2 * j + 1] + smooth[2 * j + 2]
        pair[j, 0], pair[j, 1] = total[:, 0:128], total[:, 128:256]
        defect = [
            d[i + 2] - operator(smooth[i + 1], smooth[i], smooth[i + 2], 1.0) for i in (2 * j, 2 * j + 1)
        ]
        total = defect[0] + defect[1]
        pair[j + 2, 0], pair[j + 2, 1] = total[:, 0:128], total[:, 128:256]
    for j in range(4):
        for k in range(2):
            total = pair[j, k, pl.ds(8, 16, stride=2)] + pair[j, k, pl.ds(9, 16, stride=2)]
            rows[16 * j : 16 * j + 16, 128 * k : 128 * k + 128] = total
    third = lax.broadcasted_iota(jnp.int32, (256, 128), 0)
    half = lax.broadcasted_iota(jnp.int32, (256, 128), 1)
    weights = jnp.where(third // 2 == half, 0.125, 0.0).astype(jnp.bfloat16)
    coarse[...] = exact_dot(rows[...], weights).reshape(4, 16, 128)
    for face, layer in ((up, 3), (down, 2)):
        for j in range(4):
            at, lane = 8 + 16 * (j // 2), 128 * (j % 2)
            face[j] = smooth[layer, at : at + 16, lane : lane + 128]


def coarse_kernel(
    smooth, dens, own, flo, fhi, nlo, nhi, yrows, zrows,
    out, a, r, g, c0, c1, wide, corrected, post,
):
    def place(rows, mine, far_low, far_high, low, high):
        for ref, at in ((a, 0), (r, 1)):
            ref[0:1, rows] = low[at : at + 1]
            ref[1:3, rows] = far_low[2 * at : 2 * at + 2]
            ref[3:5, rows] = high[2 * at + 6 : 2 * at + 8]
            ref[5:7, rows] = low[2 * at + 2 : 2 * at + 4]
            ref[7:9, rows] = mine[2 * at : 2 * at + 2]
            ref[9:11, rows] = high[2 * at + 2 : 2 * at + 4]
            ref[11:13, rows] = low[2 * at + 6 : 2 * at + 8]
            ref[13:15, rows] = far_high[2 * at : 2 * at + 2]
            ref[15:16, rows] = high[at : at + 1]

    place(slice(8, 24), own, flo, fhi, nlo, nhi)
    for rows, side in ((slice(0, 8), yrows), (slice(24, 32), zrows)):
        place(rows, side.at[0:4], side.at[4:8], side.at[8:12], side.at[12:22], side.at[22:32])
    for i in range(16):
        v = a[i]
        c0[i] = v - r[i] / ((1.5 + mass) / damping + (mass / damping) * (v * v))
    for i in range(1, 15):
        g[i] = operator(a[i], a[i - 1], a[i + 1], 0.25) + r[i]
    now, later = c0, c1
    for sweep in range(1, 6):
        for i in range(sweep, 16 - sweep):
            later[i] = jacobi(now[i], now[i - 1], now[i + 1], g[i], 0.25)
        now, later = later, now
    change = (now[5:11] - a[5:11]).reshape(192, 128)
    half = lax.broadcasted_iota(jnp.int32, (128, 256), 0)
    third = lax.broadcasted_iota(jnp.int32, (128, 256), 1)
    beside = (third // 2 + 2 * (third % 2) - 1 + 128) % 128
    weights = jnp.where(third // 2 == half, 0.75, jnp.where(beside == half, 0.25, 0.0)).astype(jnp.bfloat16)
    spread = exact_dot(change, weights).reshape(6, 32, 256)
    for i in range(6):
        v = spread[i]
        even = 0.75 * v + 0.25 * pltpu.roll(v, 1, 0)
        odd = 0.75 * v + 0.25 * pltpu.roll(v, 31, 0)
        for k in range(2):
            wide[i, k, pl.ds(0, 32, stride=2)] = even[:, 128 * k : 128 * k + 128]
            wide[i, k, pl.ds(1, 32, stride=2)] = odd[:, 128 * k : 128 * k + 128]
    for j in range(4):
        at, lane = 8 + 16 * (j // 2), 128 * (j % 2)
        corrected[0, at : at + 16, lane : lane + 128] = nlo[10 + j]
        corrected[7, at : at + 16, lane : lane + 128] = nhi[10 + j]
    for i in range(8):
        near = i // 2 + 1
        beside_layer = near - 1 if i % 2 == 0 else near + 1
        before = corrected.at[i] if i in (0, 7) else smooth.at[i - 1]
        for k in range(2):
            lanes = slice(128 * k, 128 * k + 128)
            change = 0.75 * wide[near, k, 8:56] + 0.25 * wide[beside_layer, k, 8:56]
            corrected[i, :, lanes] = before[:, lanes] + change
    for i in range(6):
        post[i] = jacobi(corrected[i + 1], corrected[i], corrected[i + 2], dens[i], 1.0)
    for i in range(4):
        out[i] = jacobi(post[i + 1], post[i], post[i + 2], dens[i + 1], 1.0)[8:40]


def call(kernel, outs, scratch, *args):
    vmem = pl.BlockSpec(memory_space=pltpu.VMEM)
    shapes = [jax.ShapeDtypeStruct(shape, jnp.float32) for shape in outs]
    return pl.pallas_call(
        kernel,
        out_shape=shapes,
        in_specs=[vmem] * len(args),
        out_specs=[vmem] * len(outs),
        scratch_shapes=[pltpu.VMEM(shape, jnp.float32) for shape in scratch],
        compiler_params=pltpu.CompilerParams(vmem_limit_bytes=32 * 1024 * 1024),
    )(*args)


def send(values, axis, step):
    count = lax.axis_size(axis)
    return lax.ppermute(values, axis, [(i, (i + step) % count) for i in range(count)])


def rows_from_sides(pieces):
    last = jnp.concatenate([piece[:, 8:16] for piece in pieces], 0)
    first = jnp.concatenate([piece[:, 0:8] for piece in pieces], 0)
    return send(last, "gy", 1), send(first, "gy", -1)


def body(density, field):
    xlo = send(jnp.concatenate([field[1:4], density[2:4]], 0), "gx", 1)
    xhi = send(jnp.concatenate([field[0:3], density[0:2]], 0), "gx", -1)
    clo = send(jnp.concatenate([xlo[:, 28:32], xhi[:, 28:32], field[:, 28:32], density[:, 28:32]], 0), "gy", 1)
    chi = send(jnp.concatenate([xlo[:, 0:4], xhi[:, 0:4], field[:, 0:4], density[:, 0:4]], 0), "gy", -1)
    smooth, dens, own, up, down = call(
        fine_kernel,
        [(6, 48, 256), (6, 48, 256), (4, 16, 128), (4, 16, 128), (4, 16, 128)],
        [(10, 48, 256), (8, 48, 256), (8, 48, 256), (4, 2, 48, 128), (64, 256)],
        field, density, xlo, xhi, clo, chi,
    )
    flo, fhi = send(own, "gx", 3), send(own, "gx", -3)
    nlo = send(jnp.concatenate([flo[1:2], flo[3:4], own, fhi, up], 0), "gx", 1)
    nhi = send(jnp.concatenate([fhi[0:1], fhi[2:3], own, flo, down], 0), "gx", -1)
    yrows, zrows = rows_from_sides([own, flo, fhi, nlo[0:10], nhi[0:10]])
    (out,) = call(
        coarse_kernel,
        [(4, 32, 256)],
        [(16, 32, 128)] * 5 + [(6, 2, 64, 128), (8, 48, 256), (6, 48, 256)],
        smooth, dens, own, flo, fhi, nlo, nhi, yrows, zrows,
    )
    return out


def solution(mesh):
    placed = (P("gx", "gy", None), P("gx", "gy", None))
    return jax.shard_map(body, mesh=mesh, in_specs=placed, out_specs=P("gx", "gy", None), check_vma=False)
```

```python
import jax
import jax.numpy as jnp
from jax import lax
from jax.experimental import pallas as pl
from jax.experimental.pallas import tpu as pltpu
from jax.sharding import PartitionSpec as P

mass = 0.02
damping = 0.8


def jacobi(v, below, above, source, inv_step):
    around = below + above
    around = around + pltpu.roll(v, 1, 0) + pltpu.roll(v, v.shape[0] - 1, 0)
    around = around + pltpu.roll(v, 1, 1) + pltpu.roll(v, v.shape[1] - 1, 1)
    square = v * v
    top = inv_step * around - source - v * ((6.0 * inv_step + mass) + (mass / 3.0) * square)
    return v + top / ((6.0 * inv_step + mass) / damping + (mass / damping) * square)


def operator(v, below, above, inv_step):
    around = below + above
    around = around + pltpu.roll(v, 1, 0) + pltpu.roll(v, v.shape[0] - 1, 0)
    around = around + pltpu.roll(v, 1, 1) + pltpu.roll(v, v.shape[1] - 1, 1)
    return inv_step * around - v * ((6.0 * inv_step + mass) + (mass / 3.0) * (v * v))


def exact_dot(values, weights):
    high = values.astype(jnp.bfloat16)
    rest = values - high.astype(jnp.float32)
    middle = rest.astype(jnp.bfloat16)
    low = (rest - middle.astype(jnp.float32)).astype(jnp.bfloat16)
    total = jnp.dot(low, weights, preferred_element_type=jnp.float32)
    total = total + jnp.dot(middle, weights, preferred_element_type=jnp.float32)
    return total + jnp.dot(high, weights, preferred_element_type=jnp.float32)


def fine_kernel(field, density, xlo, xhi, clo, chi, smooth, dens, coarse, coarse2, up, down, f, d, s1, pair, rows):
    f[0:3, 8:40] = xlo[0:3]
    f[3:7, 8:40] = field[...]
    f[7:10, 8:40] = xhi[0:3]
    d[0:2, 8:40] = xlo[3:5]
    d[2:6, 8:40] = density[...]
    d[6:8, 8:40] = xhi[3:5]
    for side, at in ((clo, 4), (chi, 40)):
        f[0:3, at : at + 4] = side[0:3]
        f[3:7, at : at + 4] = side[10:14]
        f[7:10, at : at + 4] = side[5:8]
        d[0:2, at : at + 4] = side[3:5]
        d[2:6, at : at + 4] = side[14:18]
        d[6:8, at : at + 4] = side[8:10]
    for i in range(8):
        s1[i] = jacobi(f[i + 1], f[i], f[i + 2], d[i], 1.0)
    for i in range(6):
        smooth[i] = jacobi(s1[i + 1], s1[i], s1[i + 2], d[i + 1], 1.0)
    dens[...] = d[1:7]
    for j in range(2):
        total = smooth[2 * j + 1] + smooth[2 * j + 2]
        pair[j, 0], pair[j, 1] = total[:, 0:128], total[:, 128:256]
        defect = [
            d[i + 2] - operator(smooth[i + 1], smooth[i], smooth[i + 2], 1.0) for i in (2 * j, 2 * j + 1)
        ]
        total = defect[0] + defect[1]
        pair[j + 2, 0], pair[j + 2, 1] = total[:, 0:128], total[:, 128:256]
    for j in range(4):
        for k in range(2):
            total = pair[j, k, pl.ds(8, 16, stride=2)] + pair[j, k, pl.ds(9, 16, stride=2)]
            rows[16 * j : 16 * j + 16, 128 * k : 128 * k + 128] = total
    third = lax.broadcasted_iota(jnp.int32, (256, 128), 0)
    half = lax.broadcasted_iota(jnp.int32, (256, 128), 1)
    weights = jnp.where(third // 2 == half, 0.125, 0.0).astype(jnp.bfloat16)
    coarse[...] = exact_dot(rows[...], weights).reshape(4, 16, 128)
    coarse2[...] = coarse[...]
    for face, layer in ((up, 3), (down, 2)):
        for j in range(4):
            at, lane = 8 + 16 * (j // 2), 128 * (j % 2)
            face[j] = smooth[layer, at : at + 16, lane : lane + 128]


def coarse_kernel(
    smooth, dens, own, flo, fhi, nlo, nhi, yrows, zrows,
    out, a, r, g, c0, c1, wide, corrected, post,
):
    def place(rows, mine, far_low, far_high, low, high):
        for ref, at in ((a, 0), (r, 1)):
            ref[0:1, rows] = low[at : at + 1]
            ref[1:3, rows] = far_low[2 * at : 2 * at + 2]
            ref[3:5, rows] = high[2 * at + 6 : 2 * at + 8]
            ref[5:7, rows] = low[2 * at + 2 : 2 * at + 4]
            ref[7:9, rows] = mine[2 * at : 2 * at + 2]
            ref[9:11, rows] = high[2 * at + 2 : 2 * at + 4]
            ref[11:13, rows] = low[2 * at + 6 : 2 * at + 8]
            ref[13:15, rows] = far_high[2 * at : 2 * at + 2]
            ref[15:16, rows] = high[at : at + 1]

    place(slice(8, 24), own, flo, fhi, nlo, nhi)
    for rows, side in ((slice(0, 8), yrows), (slice(24, 32), zrows)):
        place(rows, side.at[0:4], side.at[4:8], side.at[8:12], side.at[12:22], side.at[22:32])
    for i in range(16):
        v = a[i]
        c0[i] = v - r[i] / ((1.5 + mass) / damping + (mass / damping) * (v * v))
    for i in range(1, 15):
        g[i] = operator(a[i], a[i - 1], a[i + 1], 0.25) + r[i]
    now, later = c0, c1
    for sweep in range(1, 6):
        for i in range(sweep, 16 - sweep):
            later[i] = jacobi(now[i], now[i - 1], now[i + 1], g[i], 0.25)
        now, later = later, now
    change = (now[5:11] - a[5:11]).reshape(192, 128)
    half = lax.broadcasted_iota(jnp.int32, (128, 256), 0)
    third = lax.broadcasted_iota(jnp.int32, (128, 256), 1)
    beside = (third // 2 + 2 * (third % 2) - 1 + 128) % 128
    weights = jnp.where(third // 2 == half, 0.75, jnp.where(beside == half, 0.25, 0.0)).astype(jnp.bfloat16)
    spread = exact_dot(change, weights).reshape(6, 32, 256)
    for i in range(6):
        v = spread[i]
        even = 0.75 * v + 0.25 * pltpu.roll(v, 1, 0)
        odd = 0.75 * v + 0.25 * pltpu.roll(v, 31, 0)
        for k in range(2):
            wide[i, k, pl.ds(0, 32, stride=2)] = even[:, 128 * k : 128 * k + 128]
            wide[i, k, pl.ds(1, 32, stride=2)] = odd[:, 128 * k : 128 * k + 128]
    for j in range(4):
        at, lane = 8 + 16 * (j // 2), 128 * (j % 2)
        corrected[0, at : at + 16, lane : lane + 128] = nlo[10 + j]
        corrected[7, at : at + 16, lane : lane + 128] = nhi[10 + j]
    for i in range(8):
        near = i // 2 + 1
        beside_layer = near - 1 if i % 2 == 0 else near + 1
        before = corrected.at[i] if i in (0, 7) else smooth.at[i - 1]
        for k in range(2):
            lanes = slice(128 * k, 128 * k + 128)
            change = 0.75 * wide[near, k, 8:56] + 0.25 * wide[beside_layer, k, 8:56]
            corrected[i, :, lanes] = before[:, lanes] + change
    for i in range(6):
        post[i] = jacobi(corrected[i + 1], corrected[i], corrected[i + 2], dens[i], 1.0)
    for i in range(4):
        out[i] = jacobi(post[i + 1], post[i], post[i + 2], dens[i + 1], 1.0)[8:40]


def call(kernel, outs, scratch, *args):
    vmem = pl.BlockSpec(memory_space=pltpu.VMEM)
    shapes = [jax.ShapeDtypeStruct(shape, jnp.float32) for shape in outs]
    return pl.pallas_call(
        kernel,
        out_shape=shapes,
        in_specs=[vmem] * len(args),
        out_specs=[vmem] * len(outs),
        scratch_shapes=[pltpu.VMEM(shape, jnp.float32) for shape in scratch],
        compiler_params=pltpu.CompilerParams(vmem_limit_bytes=32 * 1024 * 1024),
    )(*args)


def send(values, axis, step):
    count = lax.axis_size(axis)
    return lax.ppermute(values, axis, [(i, (i + step) % count) for i in range(count)])


def rows_from_sides(pieces):
    last = jnp.concatenate([piece[:, 8:16] for piece in pieces], 0)
    first = jnp.concatenate([piece[:, 0:8] for piece in pieces], 0)
    return send(last, "gy", 1), send(first, "gy", -1)


def body(density, field):
    xlo = send(jnp.concatenate([field[1:4], density[2:4]], 0), "gx", 1)
    xhi = send(jnp.concatenate([field[0:3], density[0:2]], 0), "gx", -1)
    clo = send(jnp.concatenate([xlo[:, 28:32], xhi[:, 28:32], field[:, 28:32], density[:, 28:32]], 0), "gy", 1)
    chi = send(jnp.concatenate([xlo[:, 0:4], xhi[:, 0:4], field[:, 0:4], density[:, 0:4]], 0), "gy", -1)
    smooth, dens, own, own2, up, down = call(
        fine_kernel,
        [(6, 48, 256), (6, 48, 256), (4, 16, 128), (4, 16, 128), (4, 16, 128), (4, 16, 128)],
        [(10, 48, 256), (8, 48, 256), (8, 48, 256), (4, 2, 48, 128), (64, 256)],
        field, density, xlo, xhi, clo, chi,
    )
    flo, fhi = send(own, "gx", 3), send(own2, "gx", -3)
    nlo = send(jnp.concatenate([flo[1:2], flo[3:4], own, fhi, up], 0), "gx", 1)
    nhi = send(jnp.concatenate([fhi[0:1], fhi[2:3], own, flo, down], 0), "gx", -1)
    yrows, zrows = rows_from_sides([own, flo, fhi, nlo[0:10], nhi[0:10]])
    (out,) = call(
        coarse_kernel,
        [(4, 32, 256)],
        [(16, 32, 128)] * 5 + [(6, 2, 64, 128), (8, 48, 256), (6, 48, 256)],
        smooth, dens, own, flo, fhi, nlo, nhi, yrows, zrows,
    )
    return out


def solution(mesh):
    placed = (P("gx", "gy", None), P("gx", "gy", None))
    return jax.shard_map(body, mesh=mesh, in_specs=placed, out_specs=P("gx", "gy", None), check_vma=False)
```

```python
import jax
import jax.numpy as jnp
from jax import lax
from jax.experimental import pallas as pl
from jax.experimental.pallas import tpu as pltpu
from jax.sharding import PartitionSpec as P

mass = 0.02
damping = 0.8


def jacobi(v, below, above, source, inv_step):
    around = below + above
    around = around + pltpu.roll(v, 1, 0) + pltpu.roll(v, v.shape[0] - 1, 0)
    around = around + pltpu.roll(v, 1, 1) + pltpu.roll(v, v.shape[1] - 1, 1)
    square = v * v
    top = inv_step * around - source - v * ((6.0 * inv_step + mass) + (mass / 3.0) * square)
    return v + top / ((6.0 * inv_step + mass) / damping + (mass / damping) * square)


def operator(v, below, above, inv_step):
    around = below + above
    around = around + pltpu.roll(v, 1, 0) + pltpu.roll(v, v.shape[0] - 1, 0)
    around = around + pltpu.roll(v, 1, 1) + pltpu.roll(v, v.shape[1] - 1, 1)
    return inv_step * around - v * ((6.0 * inv_step + mass) + (mass / 3.0) * (v * v))


def exact_dot(values, weights):
    high = values.astype(jnp.bfloat16)
    rest = values - high.astype(jnp.float32)
    middle = rest.astype(jnp.bfloat16)
    low = (rest - middle.astype(jnp.float32)).astype(jnp.bfloat16)
    total = jnp.dot(low, weights, preferred_element_type=jnp.float32)
    total = total + jnp.dot(middle, weights, preferred_element_type=jnp.float32)
    return total + jnp.dot(high, weights, preferred_element_type=jnp.float32)


def fine_kernel(field, density, xhi, xlo, clo, chi, smooth, dens, coarse, coarse2, up, down, f, d, s1, pair, rows):
    f[0:3, 8:40] = xlo[0:3]
    f[3:7, 8:40] = field[...]
    f[7:10, 8:40] = xhi[0:3]
    d[0:2, 8:40] = xlo[3:5]
    d[2:6, 8:40] = density[...]
    d[6:8, 8:40] = xhi[3:5]
    for side, at in ((clo, 4), (chi, 40)):
        f[0:3, at : at + 4] = side[0:3]
        f[3:7, at : at + 4] = side[10:14]
        f[7:10, at : at + 4] = side[5:8]
        d[0:2, at : at + 4] = side[3:5]
        d[2:6, at : at + 4] = side[14:18]
        d[6:8, at : at + 4] = side[8:10]
    for i in range(8):
        s1[i] = jacobi(f[i + 1], f[i], f[i + 2], d[i], 1.0)
    for i in range(6):
        smooth[i] = jacobi(s1[i + 1], s1[i], s1[i + 2], d[i + 1], 1.0)
    dens[...] = d[1:7]
    for j in range(2):
        total = smooth[2 * j + 1] + smooth[2 * j + 2]
        pair[j, 0], pair[j, 1] = total[:, 0:128], total[:, 128:256]
        defect = [
            d[i + 2] - operator(smooth[i + 1], smooth[i], smooth[i + 2], 1.0) for i in (2 * j, 2 * j + 1)
        ]
        total = defect[0] + defect[1]
        pair[j + 2, 0], pair[j + 2, 1] = total[:, 0:128], total[:, 128:256]
    for j in range(4):
        for k in range(2):
            total = pair[j, k, pl.ds(8, 16, stride=2)] + pair[j, k, pl.ds(9, 16, stride=2)]
            rows[16 * j : 16 * j + 16, 128 * k : 128 * k + 128] = total
    third = lax.broadcasted_iota(jnp.int32, (256, 128), 0)
    half = lax.broadcasted_iota(jnp.int32, (256, 128), 1)
    weights = jnp.where(third >> 1 == half, 0.125, 0.0).astype(jnp.bfloat16)
    coarse[...] = exact_dot(rows[...], weights).reshape(4, 16, 128)
    coarse2[...] = coarse[...]
    for face, layer in ((up, 3), (down, 2)):
        for j in range(4):
            at, lane = 8 + 16 * (j // 2), 128 * (j % 2)
            face[j] = smooth[layer, at : at + 16, lane : lane + 128]


def coarse_kernel(
    smooth, dens, own, flo, fhi, nlo, nhi, yrows, zrows,
    out, a, r, g, c0, c1, wide, corrected, post,
):
    def place(rows, mine, far_low, far_high, low, high):
        for ref, at in ((a, 0), (r, 1)):
            ref[0:1, rows] = low[at : at + 1]
            ref[1:3, rows] = far_low[2 * at : 2 * at + 2]
            ref[3:5, rows] = high[2 * at + 6 : 2 * at + 8]
            ref[5:7, rows] = low[2 * at + 2 : 2 * at + 4]
            ref[7:9, rows] = mine[2 * at : 2 * at + 2]
            ref[9:11, rows] = high[2 * at + 2 : 2 * at + 4]
            ref[11:13, rows] = low[2 * at + 6 : 2 * at + 8]
            ref[13:15, rows] = far_high[2 * at : 2 * at + 2]
            ref[15:16, rows] = high[at : at + 1]

    place(slice(8, 24), own, flo, fhi, nlo, nhi)
    for rows, side in ((slice(0, 8), yrows), (slice(24, 32), zrows)):
        place(rows, side.at[0:4], side.at[4:8], side.at[8:12], side.at[12:22], side.at[22:32])
    for i in range(16):
        v = a[i]
        c0[i] = v - r[i] / ((1.5 + mass) / damping + (mass / damping) * (v * v))
    for i in range(1, 15):
        g[i] = operator(a[i], a[i - 1], a[i + 1], 0.25) + r[i]
    now, later = c0, c1
    for sweep in range(1, 6):
        for i in range(sweep, 16 - sweep):
            later[i] = jacobi(now[i], now[i - 1], now[i + 1], g[i], 0.25)
        now, later = later, now
    change = (now[5:11] - a[5:11]).reshape(192, 128)
    half = lax.broadcasted_iota(jnp.int32, (128, 256), 0)
    third = lax.broadcasted_iota(jnp.int32, (128, 256), 1)
    beside = ((third >> 1) + 2 * (third & 1) - 1) & 127
    weights = jnp.where(third >> 1 == half, 0.75, jnp.where(beside == half, 0.25, 0.0)).astype(jnp.bfloat16)
    spread = exact_dot(change, weights).reshape(6, 32, 256)
    for i in range(6):
        v = spread[i]
        even = 0.75 * v + 0.25 * pltpu.roll(v, 1, 0)
        odd = 0.75 * v + 0.25 * pltpu.roll(v, 31, 0)
        for k in range(2):
            wide[i, k, pl.ds(0, 32, stride=2)] = even[:, 128 * k : 128 * k + 128]
            wide[i, k, pl.ds(1, 32, stride=2)] = odd[:, 128 * k : 128 * k + 128]
    for j in range(4):
        at, lane = 8 + 16 * (j // 2), 128 * (j % 2)
        corrected[0, at : at + 16, lane : lane + 128] = nlo[10 + j]
        corrected[7, at : at + 16, lane : lane + 128] = nhi[10 + j]
    for i in range(8):
        near = i // 2 + 1
        beside_layer = near - 1 if i % 2 == 0 else near + 1
        before = corrected.at[i] if i in (0, 7) else smooth.at[i - 1]
        for k in range(2):
            lanes = slice(128 * k, 128 * k + 128)
            change = 0.75 * wide[near, k, 8:56] + 0.25 * wide[beside_layer, k, 8:56]
            corrected[i, :, lanes] = before[:, lanes] + change
    for i in range(6):
        post[i] = jacobi(corrected[i + 1], corrected[i], corrected[i + 2], dens[i], 1.0)
    for i in range(4):
        out[i] = jacobi(post[i + 1], post[i], post[i + 2], dens[i + 1], 1.0)[8:40]


def call(kernel, outs, scratch, *args):
    vmem = pl.BlockSpec(memory_space=pltpu.VMEM)
    shapes = [jax.ShapeDtypeStruct(shape, jnp.float32) for shape in outs]
    return pl.pallas_call(
        kernel,
        out_shape=shapes,
        in_specs=[vmem] * len(args),
        out_specs=[vmem] * len(outs),
        scratch_shapes=[pltpu.VMEM(shape, jnp.float32) for shape in scratch],
        compiler_params=pltpu.CompilerParams(vmem_limit_bytes=32 * 1024 * 1024),
    )(*args)


def send(values, axis, step):
    count = lax.axis_size(axis)
    return lax.ppermute(values, axis, [(i, (i + step) % count) for i in range(count)])


def rows_from_sides(pieces):
    last = jnp.concatenate([piece[:, 8:16] for piece in pieces], 0)
    first = jnp.concatenate([piece[:, 0:8] for piece in pieces], 0)
    return send(last, "gy", 1), send(first, "gy", -1)


def body(density, field):
    xlo = send(jnp.concatenate([field[1:4], density[2:4]], 0), "gx", 1)
    xhi = send(jnp.concatenate([field[0:3], density[0:2]], 0), "gx", -1)
    clo = send(jnp.concatenate([xlo[:, 28:32], xhi[:, 28:32], field[:, 28:32], density[:, 28:32]], 0), "gy", 1)
    chi = send(jnp.concatenate([xlo[:, 0:4], xhi[:, 0:4], field[:, 0:4], density[:, 0:4]], 0), "gy", -1)
    smooth, dens, own, own2, up, down = call(
        fine_kernel,
        [(6, 48, 256), (6, 48, 256), (4, 16, 128), (4, 16, 128), (4, 16, 128), (4, 16, 128)],
        [(10, 48, 256), (8, 48, 256), (8, 48, 256), (4, 2, 48, 128), (64, 256)],
        field, density, xhi, xlo, clo, chi,
    )
    flo, fhi = send(own, "gx", 3), send(own2, "gx", -3)
    nlo = send(jnp.concatenate([flo[1:2], flo[3:4], own, fhi, up], 0), "gx", 1)
    nhi = send(jnp.concatenate([fhi[0:1], fhi[2:3], own, flo, down], 0), "gx", -1)
    yrows, zrows = rows_from_sides([own, flo, fhi, nlo[0:10], nhi[0:10]])
    (out,) = call(
        coarse_kernel,
        [(4, 32, 256)],
        [(16, 32, 128)] * 5 + [(6, 2, 64, 128), (8, 48, 256), (6, 48, 256)],
        smooth, dens, own, flo, fhi, nlo, nhi, yrows, zrows,
    )
    return out


def solution(mesh):
    placed = (P("gx", "gy", None), P("gx", "gy", None))
    return jax.shard_map(body, mesh=mesh, in_specs=placed, out_specs=P("gx", "gy", None), check_vma=False)
```

```python
import jax
import jax.numpy as jnp
from jax import lax
from jax.experimental import pallas as pl
from jax.experimental.pallas import tpu as pltpu
from jax.sharding import PartitionSpec as P

mass = 0.02
damping = 0.8


def pair_of(ref, i, start, rows):
    return ref[i, start - 1 : start - 1 + rows] + ref[i, start + 1 : start + 1 + rows]


def jacobi_rows(v, rows, below, above, source, inv_step):
    around = below + above + rows
    around = around + pltpu.roll(v, 1, 1) + pltpu.roll(v, v.shape[1] - 1, 1)
    square = v * v
    top = inv_step * around - source - v * ((6.0 * inv_step + mass) + (mass / 3.0) * square)
    return v + top / ((6.0 * inv_step + mass) / damping + (mass / damping) * square)


def jacobi(v, below, above, source, inv_step):
    around = below + above
    around = around + pltpu.roll(v, 1, 0) + pltpu.roll(v, v.shape[0] - 1, 0)
    around = around + pltpu.roll(v, 1, 1) + pltpu.roll(v, v.shape[1] - 1, 1)
    square = v * v
    top = inv_step * around - source - v * ((6.0 * inv_step + mass) + (mass / 3.0) * square)
    return v + top / ((6.0 * inv_step + mass) / damping + (mass / damping) * square)


def operator(v, below, above, inv_step):
    around = below + above
    around = around + pltpu.roll(v, 1, 0) + pltpu.roll(v, v.shape[0] - 1, 0)
    around = around + pltpu.roll(v, 1, 1) + pltpu.roll(v, v.shape[1] - 1, 1)
    return inv_step * around - v * ((6.0 * inv_step + mass) + (mass / 3.0) * (v * v))


def exact_dot(values, weights):
    high = values.astype(jnp.bfloat16)
    rest = values - high.astype(jnp.float32)
    middle = rest.astype(jnp.bfloat16)
    low = (rest - middle.astype(jnp.float32)).astype(jnp.bfloat16)
    total = jnp.dot(low, weights, preferred_element_type=jnp.float32)
    total = total + jnp.dot(middle, weights, preferred_element_type=jnp.float32)
    return total + jnp.dot(high, weights, preferred_element_type=jnp.float32)


def edge_kernel(field, density, backward, first, last):
    backward[0:3] = field[0:3]
    backward[3:5] = density[0:2]
    for target, at in ((first, 0), (last, 28)):
        target[0:3] = field[0:3, at : at + 4]
        target[3:5] = density[0:2, at : at + 4]


def fine_kernel(field, density, xlo, xhi, clo, chi, smooth, dens, coarse, coarse2, up, down, f, d, s1, pair, rows):
    f[0:3, 8:40] = xlo[0:3]
    f[3:7, 8:40] = field[...]
    f[7:10, 4:44] = xhi[0:3]
    d[0:2, 8:40] = xlo[3:5]
    d[2:6, 8:40] = density[...]
    d[6:8, 4:44] = xhi[3:5]
    for side, at in ((clo, 4), (chi, 40)):
        f[0:3, at : at + 4] = side[0:3]
        f[3:7, at : at + 4] = side[5:9]
        d[0:2, at : at + 4] = side[3:5]
        d[2:6, at : at + 4] = side[9:13]
    for i in range(8):
        s1[i] = jacobi(f[i + 1], f[i], f[i + 2], d[i], 1.0)
    for i in range(6):
        smooth[i] = jacobi(s1[i + 1], s1[i], s1[i + 2], d[i + 1], 1.0)
    dens[...] = d[1:7]
    for j in range(2):
        total = smooth[2 * j + 1] + smooth[2 * j + 2]
        pair[j, 0], pair[j, 1] = total[:, 0:128], total[:, 128:256]
        defect = [
            d[i + 2] - operator(smooth[i + 1], smooth[i], smooth[i + 2], 1.0) for i in (2 * j, 2 * j + 1)
        ]
        total = defect[0] + defect[1]
        pair[j + 2, 0], pair[j + 2, 1] = total[:, 0:128], total[:, 128:256]
    for j in range(4):
        for k in range(2):
            total = pair[j, k, pl.ds(8, 16, stride=2)] + pair[j, k, pl.ds(9, 16, stride=2)]
            rows[16 * j : 16 * j + 16, 128 * k : 128 * k + 128] = total
    third = lax.broadcasted_iota(jnp.int32, (256, 128), 0)
    half = lax.broadcasted_iota(jnp.int32, (256, 128), 1)
    weights = jnp.where(third >> 1 == half, 0.125, 0.0).astype(jnp.bfloat16)
    coarse[...] = exact_dot(rows[...], weights).reshape(4, 16, 128)
    coarse2[...] = coarse[...]
    for face, layer in ((up, 3), (down, 2)):
        for j in range(4):
            at, lane = 8 + 16 * (j // 2), 128 * (j % 2)
            face[j] = smooth[layer, at : at + 16, lane : lane + 128]


def coarse_kernel(
    smooth, dens, own, flo, fhi, nlo, nhi, yrows, zrows,
    out, a, r, g, c0, c1, wide, corrected, post,
):
    def place(rows, mine, far_low, far_high, low, high):
        for ref, at in ((a, 0), (r, 1)):
            ref[0:1, rows] = low[at : at + 1]
            ref[1:3, rows] = far_low[2 * at : 2 * at + 2]
            ref[3:5, rows] = high[2 * at + 6 : 2 * at + 8]
            ref[5:7, rows] = low[2 * at + 2 : 2 * at + 4]
            ref[7:9, rows] = mine[2 * at : 2 * at + 2]
            ref[9:11, rows] = high[2 * at + 2 : 2 * at + 4]
            ref[11:13, rows] = low[2 * at + 6 : 2 * at + 8]
            ref[13:15, rows] = far_high[2 * at : 2 * at + 2]
            ref[15:16, rows] = high[at : at + 1]

    place(slice(8, 24), own, flo, fhi, nlo, nhi)
    for rows, side in ((slice(0, 8), yrows), (slice(24, 32), zrows)):
        place(rows, side.at[0:4], side.at[4:8], side.at[8:12], side.at[12:22], side.at[22:32])
    for i in range(16):
        v = a[i]
        c0[i, 8:40] = v - r[i] / ((1.5 + mass) / damping + (mass / damping) * (v * v))
    for i in range(1, 15):
        g[i] = operator(a[i], a[i - 1], a[i + 1], 0.25) + r[i]
    now, later = c0, c1
    for sweep in range(1, 6):
        for i in range(sweep, 16 - sweep):
            later[i, 8:40] = jacobi_rows(now[i, 8:40], pair_of(now, i, 8, 32), now[i - 1, 8:40], now[i + 1, 8:40], g[i], 0.25)
        now, later = later, now
    change = (now[5:11, 8:40] - a[5:11]).reshape(192, 128)
    half = lax.broadcasted_iota(jnp.int32, (128, 256), 0)
    third = lax.broadcasted_iota(jnp.int32, (128, 256), 1)
    beside = ((third >> 1) + 2 * (third & 1) - 1) & 127
    weights = jnp.where(third >> 1 == half, 0.75, jnp.where(beside == half, 0.25, 0.0)).astype(jnp.bfloat16)
    spread = exact_dot(change, weights).reshape(6, 32, 256)
    for i in range(6):
        v = spread[i]
        even = 0.75 * v + 0.25 * pltpu.roll(v, 1, 0)
        odd = 0.75 * v + 0.25 * pltpu.roll(v, 31, 0)
        for k in range(2):
            wide[i, k, pl.ds(0, 32, stride=2)] = even[:, 128 * k : 128 * k + 128]
            wide[i, k, pl.ds(1, 32, stride=2)] = odd[:, 128 * k : 128 * k + 128]
    for j in range(4):
        at, lane = 8 + 16 * (j // 2), 128 * (j % 2)
        corrected[0, at : at + 16, lane : lane + 128] = nlo[10 + j]
        corrected[7, at : at + 16, lane : lane + 128] = nhi[10 + j]
    for i in range(8):
        near = i // 2 + 1
        beside_layer = near - 1 if i % 2 == 0 else near + 1
        before = corrected.at[i] if i in (0, 7) else smooth.at[i - 1]
        for k in range(2):
            lanes = slice(128 * k, 128 * k + 128)
            change = 0.75 * wide[near, k, 8:56] + 0.25 * wide[beside_layer, k, 8:56]
            corrected[i, :, lanes] = before[:, lanes] + change
    for i in range(6):
        post[i] = jacobi(corrected[i + 1], corrected[i], corrected[i + 2], dens[i], 1.0)
    for i in range(4):
        out[i] = jacobi(post[i + 1], post[i], post[i + 2], dens[i + 1], 1.0)[8:40]


def call(kernel, outs, scratch, *args):
    vmem = pl.BlockSpec(memory_space=pltpu.VMEM)
    shapes = [jax.ShapeDtypeStruct(shape, jnp.float32) for shape in outs]
    return pl.pallas_call(
        kernel,
        out_shape=shapes,
        in_specs=[vmem] * len(args),
        out_specs=[vmem] * len(outs),
        scratch_shapes=[pltpu.VMEM(shape, jnp.float32) for shape in scratch],
        compiler_params=pltpu.CompilerParams(vmem_limit_bytes=32 * 1024 * 1024),
    )(*args)


def send(values, axis, step):
    count = lax.axis_size(axis)
    return lax.ppermute(values, axis, [(i, (i + step) % count) for i in range(count)])


def send_both(values, step, side_step):
    count, sides = lax.axis_size("gx"), lax.axis_size("gy")
    pairs = [
        (i * sides + j, (i + step) % count * sides + (j + side_step) % sides) for i in range(count) for j in range(sides)
    ]
    return lax.ppermute(values, ("gx", "gy"), pairs)


def rows_from_sides(pieces):
    last = jnp.concatenate([piece[:, 8:16] for piece in pieces], 0)
    first = jnp.concatenate([piece[:, 0:8] for piece in pieces], 0)
    return send(last, "gy", 1), send(first, "gy", -1)


def body(density, field):
    xlo = send(jnp.concatenate([field[1:4], density[2:4]], 0), "gx", 1)
    backward, first, last = pl.pallas_call(
        edge_kernel,
        out_shape=[jax.ShapeDtypeStruct((5, rows, 256), jnp.float32) for rows in (32, 4, 4)],
        in_specs=[pl.BlockSpec(memory_space=pltpu.VMEM)] * 2,
        out_specs=[pl.BlockSpec(memory_space=pltpu.VMEM)] * 3,
    )(field, density)
    dlo = send_both(last, -1, 1)
    dhi = send_both(first, -1, -1)
    xhi = send(backward, "gx", -1)
    xhi = jnp.concatenate([dlo, xhi, dhi], 1)
    clo = send(jnp.concatenate([xlo[:, 28:32], field[:, 28:32], density[:, 28:32]], 0), "gy", 1)
    chi = send(jnp.concatenate([xlo[:, 0:4], field[:, 0:4], density[:, 0:4]], 0), "gy", -1)
    smooth, dens, own, own2, up, down = call(
        fine_kernel,
        [(6, 48, 256), (6, 48, 256), (4, 16, 128), (4, 16, 128), (4, 16, 128), (4, 16, 128)],
        [(10, 48, 256), (8, 48, 256), (8, 48, 256), (4, 2, 48, 128), (64, 256)],
        field, density, xlo, xhi, clo, chi,
    )
    flo, fhi = send(own, "gx", 3), send(own2, "gx", -3)
    nlo = send(jnp.concatenate([flo[1:2], flo[3:4], own, fhi, up], 0), "gx", 1)
    nhi = send(jnp.concatenate([fhi[0:1], fhi[2:3], own, flo, down], 0), "gx", -1)
    yrows, zrows = rows_from_sides([own, flo, fhi, nlo[0:10], nhi[0:10]])
    (out,) = call(
        coarse_kernel,
        [(4, 32, 256)],
        [(16, 32, 128)] * 3 + [(16, 48, 128)] * 2 + [(6, 2, 64, 128), (8, 48, 256), (6, 48, 256)],
        smooth, dens, own, flo, fhi, nlo, nhi, yrows, zrows,
    )
    return out


def solution(mesh):
    placed = (P("gx", "gy", None), P("gx", "gy", None))
    return jax.shard_map(body, mesh=mesh, in_specs=placed, out_specs=P("gx", "gy", None), check_vma=False)
```

```python
import jax
import jax.numpy as jnp
from jax import lax
from jax.experimental import pallas as pl
from jax.experimental.pallas import tpu as pltpu
from jax.sharding import PartitionSpec as P

mass = 0.02
damping = 0.8


def pair_of(ref, i, start, rows):
    return ref[i, start - 1 : start - 1 + rows] + ref[i, start + 1 : start + 1 + rows]


def jacobi_rows(v, rows, below, above, source, inv_step):
    around = below + above + rows
    around = around + pltpu.roll(v, 1, 1) + pltpu.roll(v, v.shape[1] - 1, 1)
    square = v * v
    top = inv_step * around - source - v * ((6.0 * inv_step + mass) + (mass / 3.0) * square)
    return v + top / ((6.0 * inv_step + mass) / damping + (mass / damping) * square)


def jacobi(v, below, above, source, inv_step):
    around = below + above
    around = around + pltpu.roll(v, 1, 0) + pltpu.roll(v, v.shape[0] - 1, 0)
    around = around + pltpu.roll(v, 1, 1) + pltpu.roll(v, v.shape[1] - 1, 1)
    square = v * v
    top = inv_step * around - source - v * ((6.0 * inv_step + mass) + (mass / 3.0) * square)
    return v + top / ((6.0 * inv_step + mass) / damping + (mass / damping) * square)


def operator(v, below, above, inv_step):
    around = below + above
    around = around + pltpu.roll(v, 1, 0) + pltpu.roll(v, v.shape[0] - 1, 0)
    around = around + pltpu.roll(v, 1, 1) + pltpu.roll(v, v.shape[1] - 1, 1)
    return inv_step * around - v * ((6.0 * inv_step + mass) + (mass / 3.0) * (v * v))


def exact_dot(values, weights):
    high = values.astype(jnp.bfloat16)
    rest = values - high.astype(jnp.float32)
    middle = rest.astype(jnp.bfloat16)
    low = (rest - middle.astype(jnp.float32)).astype(jnp.bfloat16)
    total = jnp.dot(low, weights, preferred_element_type=jnp.float32)
    total = total + jnp.dot(middle, weights, preferred_element_type=jnp.float32)
    return total + jnp.dot(high, weights, preferred_element_type=jnp.float32)


def fine_kernel(field, density, xlo, xhi, clo, chi, smooth, dens, forward, backward, f, d, s1, pair, rows):
    f[0:3, 8:40] = xlo[0:3]
    f[3:7, 8:40] = field[...]
    f[7:10, 8:40] = xhi[0:3]
    d[0:2, 8:40] = xlo[3:5]
    d[2:6, 8:40] = density[...]
    d[6:8, 8:40] = xhi[3:5]
    for side, at in ((clo, 4), (chi, 40)):
        f[0:3, at : at + 4] = side[0:3]
        f[3:7, at : at + 4] = side[10:14]
        f[7:10, at : at + 4] = side[5:8]
        d[0:2, at : at + 4] = side[3:5]
        d[2:6, at : at + 4] = side[14:18]
        d[6:8, at : at + 4] = side[8:10]
    for i in range(8):
        s1[i] = jacobi(f[i + 1], f[i], f[i + 2], d[i], 1.0)
    for i in range(6):
        smooth[i] = jacobi(s1[i + 1], s1[i], s1[i + 2], d[i + 1], 1.0)
    dens[...] = d[1:7]
    for j in range(2):
        total = smooth[2 * j + 1] + smooth[2 * j + 2]
        pair[j, 0], pair[j, 1] = total[:, 0:128], total[:, 128:256]
        defect = [
            d[i + 2] - operator(smooth[i + 1], smooth[i], smooth[i + 2], 1.0) for i in (2 * j, 2 * j + 1)
        ]
        total = defect[0] + defect[1]
        pair[j + 2, 0], pair[j + 2, 1] = total[:, 0:128], total[:, 128:256]
    for j in range(4):
        for k in range(2):
            total = pair[j, k, pl.ds(8, 16, stride=2)] + pair[j, k, pl.ds(9, 16, stride=2)]
            rows[16 * j : 16 * j + 16, 128 * k : 128 * k + 128] = total
    third = lax.broadcasted_iota(jnp.int32, (256, 128), 0)
    half = lax.broadcasted_iota(jnp.int32, (256, 128), 1)
    weights = jnp.where(third >> 1 == half, 0.125, 0.0).astype(jnp.bfloat16)
    coarse = exact_dot(rows[...], weights).reshape(4, 16, 128)
    forward[0:4] = coarse
    backward[0:4] = coarse
    for target, layer in ((forward, 3), (backward, 2)):
        for j in range(4):
            at, lane = 8 + 16 * (j // 2), 128 * (j % 2)
            target[4 + j] = smooth[layer, at : at + 16, lane : lane + 128]


def coarse_kernel(
    smooth, dens, own, nlo, nhi, flo, fhi, yrows, zrows,
    out, a, r, g, c0, c1, wide, corrected, post,
):
    def place(rows, mine, low, high, far_low, far_high):
        for ref, at in ((a, 0), (r, 1)):
            ref[0:1, rows] = far_low[at : at + 1]
            ref[1:3, rows] = far_low[2 * at + 2 : 2 * at + 4]
            ref[3:5, rows] = far_low[2 * at + 6 : 2 * at + 8]
            ref[5:7, rows] = low[2 * at : 2 * at + 2]
            ref[7:9, rows] = mine[2 * at : 2 * at + 2]
            ref[9:11, rows] = high[2 * at : 2 * at + 2]
            ref[11:13, rows] = far_high[2 * at + 6 : 2 * at + 8]
            ref[13:15, rows] = far_high[2 * at + 2 : 2 * at + 4]
            ref[15:16, rows] = far_high[at : at + 1]

    place(slice(8, 24), own, nlo, nhi, flo, fhi)
    for rows, side in ((slice(0, 8), yrows), (slice(24, 32), zrows)):
        place(rows, side.at[0:4], side.at[4:8], side.at[8:12], side.at[12:22], side.at[22:32])
    for i in range(16):
        v = a[i]
        c0[i, 8:40] = v - r[i] / ((1.5 + mass) / damping + (mass / damping) * (v * v))
    for i in range(1, 15):
        g[i] = operator(a[i], a[i - 1], a[i + 1], 0.25) + r[i]
    now, later = c0, c1
    for sweep in range(1, 6):
        for i in range(sweep, 16 - sweep):
            later[i, 8:40] = jacobi_rows(now[i, 8:40], pair_of(now, i, 8, 32), now[i - 1, 8:40], now[i + 1, 8:40], g[i], 0.25)
        now, later = later, now
    change = (now[5:11, 8:40] - a[5:11]).reshape(192, 128)
    half = lax.broadcasted_iota(jnp.int32, (128, 256), 0)
    third = lax.broadcasted_iota(jnp.int32, (128, 256), 1)
    beside = ((third >> 1) + 2 * (third & 1) - 1) & 127
    weights = jnp.where(third >> 1 == half, 0.75, jnp.where(beside == half, 0.25, 0.0)).astype(jnp.bfloat16)
    spread = exact_dot(change, weights).reshape(6, 32, 256)
    for i in range(6):
        v = spread[i]
        even = 0.75 * v + 0.25 * pltpu.roll(v, 1, 0)
        odd = 0.75 * v + 0.25 * pltpu.roll(v, 31, 0)
        for k in range(2):
            wide[i, k, pl.ds(0, 32, stride=2)] = even[:, 128 * k : 128 * k + 128]
            wide[i, k, pl.ds(1, 32, stride=2)] = odd[:, 128 * k : 128 * k + 128]
    for j in range(4):
        at, lane = 8 + 16 * (j // 2), 128 * (j % 2)
        corrected[0, at : at + 16, lane : lane + 128] = nlo[4 + j]
        corrected[7, at : at + 16, lane : lane + 128] = nhi[4 + j]
    for i in range(8):
        near = i // 2 + 1
        beside_layer = near - 1 if i % 2 == 0 else near + 1
        before = corrected.at[i] if i in (0, 7) else smooth.at[i - 1]
        for k in range(2):
            lanes = slice(128 * k, 128 * k + 128)
            change = 0.75 * wide[near, k, 8:56] + 0.25 * wide[beside_layer, k, 8:56]
            corrected[i, :, lanes] = before[:, lanes] + change
    for i in range(6):
        post[i] = jacobi(corrected[i + 1], corrected[i], corrected[i + 2], dens[i], 1.0)
    for i in range(4):
        out[i] = jacobi(post[i + 1], post[i], post[i + 2], dens[i + 1], 1.0)[8:40]


def call(kernel, outs, scratch, *args):
    vmem = pl.BlockSpec(memory_space=pltpu.VMEM)
    shapes = [jax.ShapeDtypeStruct(shape, jnp.float32) for shape in outs]
    return pl.pallas_call(
        kernel,
        out_shape=shapes,
        in_specs=[vmem] * len(args),
        out_specs=[vmem] * len(outs),
        scratch_shapes=[pltpu.VMEM(shape, jnp.float32) for shape in scratch],
        compiler_params=pltpu.CompilerParams(vmem_limit_bytes=32 * 1024 * 1024),
    )(*args)


def send(values, axis, step):
    count = lax.axis_size(axis)
    return lax.ppermute(values, axis, [(i, (i + step) % count) for i in range(count)])


def rows_from_sides(pieces):
    last = jnp.concatenate([piece[:, 8:16] for piece in pieces], 0)
    first = jnp.concatenate([piece[:, 0:8] for piece in pieces], 0)
    return send(last, "gy", 1), send(first, "gy", -1)


def body(density, field):
    xlo = send(jnp.concatenate([field[1:4], density[2:4]], 0), "gx", 1)
    xhi = send(jnp.concatenate([field[0:3], density[0:2]], 0), "gx", -1)
    clo = send(jnp.concatenate([xlo[:, 28:32], xhi[:, 28:32], field[:, 28:32], density[:, 28:32]], 0), "gy", 1)
    chi = send(jnp.concatenate([xlo[:, 0:4], xhi[:, 0:4], field[:, 0:4], density[:, 0:4]], 0), "gy", -1)
    smooth, dens, forward, backward = call(
        fine_kernel,
        [(6, 48, 256), (6, 48, 256), (8, 16, 128), (8, 16, 128)],
        [(10, 48, 256), (8, 48, 256), (8, 48, 256), (4, 2, 48, 128), (64, 256)],
        field, density, xlo, xhi, clo, chi,
    )
    own = forward[0:4]
    nlo, nhi = send(forward, "gx", 1), send(backward, "gx", -1)
    flo = send(jnp.concatenate([nlo[1:2], nlo[3:4], own, nhi[0:4]], 0), "gx", 3)
    own = backward[0:4]
    fhi = send(jnp.concatenate([nhi[0:1], nhi[2:3], own, nlo[0:4]], 0), "gx", -3)
    yrows, zrows = rows_from_sides([own, nlo[0:4], nhi[0:4], flo, fhi])
    (out,) = call(
        coarse_kernel,
        [(4, 32, 256)],
        [(16, 32, 128)] * 3 + [(16, 48, 128)] * 2 + [(6, 2, 64, 128), (8, 48, 256), (6, 48, 256)],
        smooth, dens, own, nlo, nhi, flo, fhi, yrows, zrows,
    )
    return out


def solution(mesh):
    placed = (P("gx", "gy", None), P("gx", "gy", None))
    return jax.shard_map(body, mesh=mesh, in_specs=placed, out_specs=P("gx", "gy", None), check_vma=False)
```

```python
import jax
import jax.numpy as jnp
from jax import lax
from jax.experimental import pallas as pl
from jax.experimental.pallas import tpu as pltpu
from jax.sharding import PartitionSpec as P

mass = 0.02
damping = 0.8


def pair_of(ref, i, start, rows):
    return ref[i, start - 1 : start - 1 + rows] + ref[i, start + 1 : start + 1 + rows]


def jacobi_rows(v, rows, below, above, source, inv_step):
    around = below + above + rows
    around = around + pltpu.roll(v, 1, 1) + pltpu.roll(v, v.shape[1] - 1, 1)
    square = v * v
    top = inv_step * around - source - v * ((6.0 * inv_step + mass) + (mass / 3.0) * square)
    return v + top / ((6.0 * inv_step + mass) / damping + (mass / damping) * square)


def jacobi(v, below, above, source, inv_step):
    around = below + above
    around = around + pltpu.roll(v, 1, 0) + pltpu.roll(v, v.shape[0] - 1, 0)
    around = around + pltpu.roll(v, 1, 1) + pltpu.roll(v, v.shape[1] - 1, 1)
    square = v * v
    top = inv_step * around - source - v * ((6.0 * inv_step + mass) + (mass / 3.0) * square)
    return v + top / ((6.0 * inv_step + mass) / damping + (mass / damping) * square)


def operator(v, below, above, inv_step):
    around = below + above
    around = around + pltpu.roll(v, 1, 0) + pltpu.roll(v, v.shape[0] - 1, 0)
    around = around + pltpu.roll(v, 1, 1) + pltpu.roll(v, v.shape[1] - 1, 1)
    return inv_step * around - v * ((6.0 * inv_step + mass) + (mass / 3.0) * (v * v))


def exact_dot(values, weights):
    high = values.astype(jnp.bfloat16)
    rest = values - high.astype(jnp.float32)
    middle = rest.astype(jnp.bfloat16)
    low = (rest - middle.astype(jnp.float32)).astype(jnp.bfloat16)
    total = jnp.dot(low, weights, preferred_element_type=jnp.float32)
    total = total + jnp.dot(middle, weights, preferred_element_type=jnp.float32)
    return total + jnp.dot(high, weights, preferred_element_type=jnp.float32)


def fine_kernel(field, density, xlo, xhi, clo, chi, smooth, dens, coarse, coarse2, up, down, f, d, s1, pair, rows):
    f[0:3, 8:40] = xlo[0:3]
    f[3:7, 8:40] = field[...]
    f[7:10, 8:40] = xhi[0:3]
    d[0:2, 8:40] = xlo[3:5]
    d[2:6, 8:40] = density[...]
    d[6:8, 8:40] = xhi[3:5]
    for side, at in ((clo, 4), (chi, 40)):
        f[0:3, at : at + 4] = side[0:3]
        f[3:7, at : at + 4] = side[10:14]
        f[7:10, at : at + 4] = side[5:8]
        d[0:2, at : at + 4] = side[3:5]
        d[2:6, at : at + 4] = side[14:18]
        d[6:8, at : at + 4] = side[8:10]
    for i in range(8):
        s1[i] = jacobi(f[i + 1], f[i], f[i + 2], d[i], 1.0)
    for i in range(6):
        smooth[i] = jacobi(s1[i + 1], s1[i], s1[i + 2], d[i + 1], 1.0)
    dens[...] = d[1:7]
    for j in range(2):
        total = smooth[2 * j + 1] + smooth[2 * j + 2]
        pair[j, 0], pair[j, 1] = total[:, 0:128], total[:, 128:256]
        defect = [
            d[i + 2] - operator(smooth[i + 1], smooth[i], smooth[i + 2], 1.0) for i in (2 * j, 2 * j + 1)
        ]
        total = defect[0] + defect[1]
        pair[j + 2, 0], pair[j + 2, 1] = total[:, 0:128], total[:, 128:256]
    for j in range(4):
        for k in range(2):
            total = pair[j, k, pl.ds(8, 16, stride=2)] + pair[j, k, pl.ds(9, 16, stride=2)]
            rows[16 * j : 16 * j + 16, 128 * k : 128 * k + 128] = total
    third = lax.broadcasted_iota(jnp.int32, (256, 128), 0)
    half = lax.broadcasted_iota(jnp.int32, (256, 128), 1)
    weights = jnp.where(third >> 1 == half, 0.125, 0.0).astype(jnp.bfloat16)
    coarse[...] = exact_dot(rows[...], weights).reshape(4, 16, 128)
    coarse2[...] = coarse[...]
    for face, layer in ((up, 3), (down, 2)):
        for j in range(4):
            at, lane = 8 + 16 * (j // 2), 128 * (j % 2)
            face[j] = smooth[layer, at : at + 16, lane : lane + 128]


def coarse_kernel(
    smooth, dens, own, flo, fhi, nlo, nhi, zrows, yrows,
    out, a, r, g, c0, c1, wide, corrected, post,
):
    for ref, at in ((a, 0), (r, 1)):
        ref[0:1, 8:24] = nlo[at : at + 1]
        ref[1:3, 8:24] = flo[2 * at : 2 * at + 2]
        ref[13:15, 8:24] = fhi[2 * at : 2 * at + 2]
        ref[15:16, 8:24] = nhi[at : at + 1]
        for rows, mine, low, high, start in (
            (slice(8, 24), own, nlo, nhi, 2),
            (slice(0, 8), yrows.at[0:4], yrows.at[4:12], yrows.at[12:20], 0),
            (slice(24, 32), zrows.at[0:4], zrows.at[4:12], zrows.at[12:20], 0),
        ):
            at_own, at_two = start + 2 * at, start + 4 + 2 * at
            ref[3:5, rows] = high[at_two : at_two + 2]
            ref[5:7, rows] = low[at_own : at_own + 2]
            ref[7:9, rows] = mine[2 * at : 2 * at + 2]
            ref[9:11, rows] = high[at_own : at_own + 2]
            ref[11:13, rows] = low[at_two : at_two + 2]
        for rows, side in ((slice(4, 8), yrows), (slice(24, 28), zrows)):
            ref[1:3, rows] = side[20 + 2 * at : 22 + 2 * at, 0:4]
            ref[0:1, rows] = side[24 + at : 25 + at, 0:4]
            ref[13:15, rows] = side[20 + 2 * at : 22 + 2 * at, 4:8]
            ref[15:16, rows] = side[24 + at : 25 + at, 4:8]
    for i in range(16):
        v = a[i]
        c0[i, 8:40] = v - r[i] / ((1.5 + mass) / damping + (mass / damping) * (v * v))
    for i in range(1, 15):
        g[i] = operator(a[i], a[i - 1], a[i + 1], 0.25) + r[i]
    now, later = c0, c1
    for sweep in range(1, 6):
        for i in range(sweep, 16 - sweep):
            later[i, 8:40] = jacobi_rows(now[i, 8:40], pair_of(now, i, 8, 32), now[i - 1, 8:40], now[i + 1, 8:40], g[i], 0.25)
        now, later = later, now
    change = (now[5:11, 8:40] - a[5:11]).reshape(192, 128)
    half = lax.broadcasted_iota(jnp.int32, (128, 256), 0)
    third = lax.broadcasted_iota(jnp.int32, (128, 256), 1)
    beside = ((third >> 1) + 2 * (third & 1) - 1) & 127
    weights = jnp.where(third >> 1 == half, 0.75, jnp.where(beside == half, 0.25, 0.0)).astype(jnp.bfloat16)
    spread = exact_dot(change, weights).reshape(6, 32, 256)
    for i in range(6):
        v = spread[i]
        even = 0.75 * v + 0.25 * pltpu.roll(v, 1, 0)
        odd = 0.75 * v + 0.25 * pltpu.roll(v, 31, 0)
        for k in range(2):
            wide[i, k, pl.ds(0, 32, stride=2)] = even[:, 128 * k : 128 * k + 128]
            wide[i, k, pl.ds(1, 32, stride=2)] = odd[:, 128 * k : 128 * k + 128]
    for j in range(4):
        at, lane = 8 + 16 * (j // 2), 128 * (j % 2)
        corrected[0, at : at + 16, lane : lane + 128] = nlo[10 + j]
        corrected[7, at : at + 16, lane : lane + 128] = nhi[10 + j]
    for i in range(8):
        near = i // 2 + 1
        beside_layer = near - 1 if i % 2 == 0 else near + 1
        before = corrected.at[i] if i in (0, 7) else smooth.at[i - 1]
        for k in range(2):
            lanes = slice(128 * k, 128 * k + 128)
            change = 0.75 * wide[near, k, 8:56] + 0.25 * wide[beside_layer, k, 8:56]
            corrected[i, :, lanes] = before[:, lanes] + change
    for i in range(6):
        post[i] = jacobi(corrected[i + 1], corrected[i], corrected[i + 2], dens[i], 1.0)
    for i in range(4):
        out[i] = jacobi(post[i + 1], post[i], post[i + 2], dens[i + 1], 1.0)[8:40]


def call(kernel, outs, scratch, *args):
    vmem = pl.BlockSpec(memory_space=pltpu.VMEM)
    shapes = [jax.ShapeDtypeStruct(shape, jnp.float32) for shape in outs]
    return pl.pallas_call(
        kernel,
        out_shape=shapes,
        in_specs=[vmem] * len(args),
        out_specs=[vmem] * len(outs),
        scratch_shapes=[pltpu.VMEM(shape, jnp.float32) for shape in scratch],
        compiler_params=pltpu.CompilerParams(vmem_limit_bytes=32 * 1024 * 1024),
    )(*args)


def send(values, axis, step):
    count = lax.axis_size(axis)
    return lax.ppermute(values, axis, [(i, (i + step) % count) for i in range(count)])


def rows_from_sides(near, far):
    last = [piece[:, 8:16] for piece in near]
    last += [jnp.concatenate([low[:, 12:16], high[:, 12:16]], 1) for low, high in far]
    first = [piece[:, 0:8] for piece in near]
    first += [jnp.concatenate([low[:, 0:4], high[:, 0:4]], 1) for low, high in far]
    return send(jnp.concatenate(last, 0), "gy", 1), send(jnp.concatenate(first, 0), "gy", -1)


def body(density, field):
    xlo = send(jnp.concatenate([field[1:4], density[2:4]], 0), "gx", 1)
    xhi = send(jnp.concatenate([field[0:3], density[0:2]], 0), "gx", -1)
    clo = send(jnp.concatenate([xlo[:, 28:32], xhi[:, 28:32], field[:, 28:32], density[:, 28:32]], 0), "gy", 1)
    chi = send(jnp.concatenate([xlo[:, 0:4], xhi[:, 0:4], field[:, 0:4], density[:, 0:4]], 0), "gy", -1)
    smooth, dens, own, own2, up, down = call(
        fine_kernel,
        [(6, 48, 256), (6, 48, 256), (4, 16, 128), (4, 16, 128), (4, 16, 128), (4, 16, 128)],
        [(10, 48, 256), (8, 48, 256), (8, 48, 256), (4, 2, 48, 128), (64, 256)],
        field, density, xlo, xhi, clo, chi,
    )
    flo, fhi = send(own, "gx", 3), send(own2, "gx", -3)
    nlo = send(jnp.concatenate([flo[1:2], flo[3:4], own, fhi, up], 0), "gx", 1)
    nhi = send(jnp.concatenate([fhi[0:1], fhi[2:3], own, flo, down], 0), "gx", -1)
    yrows, zrows = rows_from_sides([own, nlo[2:10], nhi[2:10]], [(flo, fhi), (nlo[0:2], nhi[0:2])])
    (out,) = call(
        coarse_kernel,
        [(4, 32, 256)],
        [(16, 32, 128)] * 3 + [(16, 48, 128)] * 2 + [(6, 2, 64, 128), (8, 48, 256), (6, 48, 256)],
        smooth, dens, own, flo, fhi, nlo, nhi, zrows, yrows,
    )
    return out


def solution(mesh):
    placed = (P("gx", "gy", None), P("gx", "gy", None))
    return jax.shard_map(body, mesh=mesh, in_specs=placed, out_specs=P("gx", "gy", None), check_vma=False)
```

```python
import jax
import jax.numpy as jnp
from jax import lax
from jax.experimental import pallas as pl
from jax.experimental.pallas import tpu as pltpu
from jax.sharding import PartitionSpec as P

mass = 0.02
damping = 0.8


def around(ref, i, rows):
    v, first, last = ref[i, rows], rows.start, rows.stop
    total = ref[i - 1, rows] + ref[i + 1, rows]
    total = total + (ref[i, first - 1 : last - 1] + ref[i, first + 1 : last + 1])
    return total + pltpu.roll(v, 1, 1) + pltpu.roll(v, v.shape[1] - 1, 1)


def jacobi(ref, i, rows, source, inv_step):
    v = ref[i, rows]
    square = v * v
    inner = (6.0 * inv_step + mass) + (mass / 3.0) * square
    top = inv_step * around(ref, i, rows) - source - v * inner
    return v + top / ((6.0 * inv_step + mass) / damping + (mass / damping) * square)


def operator(ref, i, rows, inv_step):
    v = ref[i, rows]
    return inv_step * around(ref, i, rows) - v * ((6.0 * inv_step + mass) + (mass / 3.0) * (v * v))


def exact_dot(values, weights):
    high = values.astype(jnp.bfloat16)
    rest = values - high.astype(jnp.float32)
    middle = rest.astype(jnp.bfloat16)
    low = (rest - middle.astype(jnp.float32)).astype(jnp.bfloat16)
    total = jnp.dot(low, weights, preferred_element_type=jnp.float32)
    total = total + jnp.dot(middle, weights, preferred_element_type=jnp.float32)
    return total + jnp.dot(high, weights, preferred_element_type=jnp.float32)


def fine_kernel(field, density, xlo, xhi, clo, chi, smooth, d, coarse, coarse2, up, down, f, s1, pair, rows):
    f[0:3, 16:48] = xlo[0:3]
    f[3:7, 16:48] = field[...]
    f[7:10, 16:48] = xhi[0:3]
    d[0:2, 8:40] = xlo[3:5]
    d[2:6, 8:40] = density[...]
    d[6:8, 8:40] = xhi[3:5]
    for side, at in ((clo, 4), (chi, 40)):
        f[0:3, at + 8 : at + 12] = side[0:3]
        f[3:7, at + 8 : at + 12] = side[10:14]
        f[7:10, at + 8 : at + 12] = side[5:8]
        d[0:2, at : at + 4] = side[3:5]
        d[2:6, at : at + 4] = side[14:18]
        d[6:8, at : at + 4] = side[8:10]
    for i in range(8):
        s1[i, 8:56] = jacobi(f, i + 1, slice(8, 56), d[i], 1.0)
    for i in range(6):
        smooth[i] = jacobi(s1, i + 1, slice(8, 56), d[i + 1], 1.0)
    for j in range(2):
        total = smooth[2 * j + 1, 8:40] + smooth[2 * j + 2, 8:40]
        pair[j, 0], pair[j, 1] = total[:, 0:128], total[:, 128:256]
        defect = [d[i + 2, 8:40] - operator(smooth, i + 1, slice(8, 40), 1.0) for i in (2 * j, 2 * j + 1)]
        total = defect[0] + defect[1]
        pair[j + 2, 0], pair[j + 2, 1] = total[:, 0:128], total[:, 128:256]
    for j in range(4):
        for k in range(2):
            total = pair[j, k, pl.ds(0, 16, stride=2)] + pair[j, k, pl.ds(1, 16, stride=2)]
            rows[16 * j : 16 * j + 16, 128 * k : 128 * k + 128] = total
    third = lax.broadcasted_iota(jnp.int32, (256, 128), 0)
    half = lax.broadcasted_iota(jnp.int32, (256, 128), 1)
    weights = jnp.where(third >> 1 == half, 0.125, 0.0).astype(jnp.bfloat16)
    coarse[...] = exact_dot(rows[...], weights).reshape(4, 16, 128)
    coarse2[...] = coarse[...]
    for face, layer in ((up, 3), (down, 2)):
        for j in range(4):
            at, lane = 8 + 16 * (j // 2), 128 * (j % 2)
            face[j] = smooth[layer, at : at + 16, lane : lane + 128]


def coarse_kernel(
    smooth, dens, own, flo, fhi, nlo, nhi, zrows, yrows,
    out, start, r, g, c0, c1, wide, corrected, post,
):
    for ref, at in ((start.at[:, 8:40], 0), (r, 1)):
        ref[0:1, 8:24] = nlo[at : at + 1]
        ref[1:3, 8:24] = flo[2 * at : 2 * at + 2]
        ref[13:15, 8:24] = fhi[2 * at : 2 * at + 2]
        ref[15:16, 8:24] = nhi[at : at + 1]
        for rows, mine, low, high, first in (
            (slice(8, 24), own, nlo, nhi, 2),
            (slice(0, 8), yrows.at[0:4], yrows.at[4:12], yrows.at[12:20], 0),
            (slice(24, 32), zrows.at[0:4], zrows.at[4:12], zrows.at[12:20], 0),
        ):
            at_own, at_two = first + 2 * at, first + 4 + 2 * at
            ref[3:5, rows] = high[at_two : at_two + 2]
            ref[5:7, rows] = low[at_own : at_own + 2]
            ref[7:9, rows] = mine[2 * at : 2 * at + 2]
            ref[9:11, rows] = high[at_own : at_own + 2]
            ref[11:13, rows] = low[at_two : at_two + 2]
        for rows, side in ((slice(4, 8), yrows), (slice(24, 28), zrows)):
            ref[1:3, rows] = side[20 + 2 * at : 22 + 2 * at, 0:4]
            ref[0:1, rows] = side[24 + at : 25 + at, 0:4]
            ref[13:15, rows] = side[20 + 2 * at : 22 + 2 * at, 4:8]
            ref[15:16, rows] = side[24 + at : 25 + at, 4:8]
    rows = slice(8, 40)
    for i in range(16):
        v = start[i, rows]
        c0[i, rows] = v - r[i] / ((1.5 + mass) / damping + (mass / damping) * (v * v))
    for i in range(1, 15):
        g[i] = operator(start, i, rows, 0.25) + r[i]
    now, later = c0, c1
    for sweep in range(1, 6):
        for i in range(sweep, 16 - sweep):
            later[i, rows] = jacobi(now, i, rows, g[i], 0.25)
        now, later = later, now
    change = (now[5:11, 8:40] - start[5:11, 8:40]).reshape(192, 128)
    half = lax.broadcasted_iota(jnp.int32, (128, 256), 0)
    third = lax.broadcasted_iota(jnp.int32, (128, 256), 1)
    beside = ((third >> 1) + 2 * (third & 1) - 1) & 127
    weights = jnp.where(third >> 1 == half, 0.75, jnp.where(beside == half, 0.25, 0.0)).astype(jnp.bfloat16)
    spread = exact_dot(change, weights).reshape(6, 32, 256)
    for i in range(6):
        v = spread[i]
        even = 0.75 * v + 0.25 * pltpu.roll(v, 1, 0)
        odd = 0.75 * v + 0.25 * pltpu.roll(v, 31, 0)
        for k in range(2):
            wide[i, k, pl.ds(0, 32, stride=2)] = even[:, 128 * k : 128 * k + 128]
            wide[i, k, pl.ds(1, 32, stride=2)] = odd[:, 128 * k : 128 * k + 128]
    for j in range(4):
        at, lane = 16 + 16 * (j // 2), 128 * (j % 2)
        corrected[0, at : at + 16, lane : lane + 128] = nlo[10 + j]
        corrected[7, at : at + 16, lane : lane + 128] = nhi[10 + j]
    for i in range(8):
        near = i // 2 + 1
        beside = near - 1 if i % 2 == 0 else near + 1
        for k in range(2):
            lanes = slice(128 * k, 128 * k + 128)
            if i in (0, 7):
                rows = slice(16, 48)
                before = corrected[i, rows, lanes]
            else:
                rows = slice(8, 56)
                before = smooth[i - 1, :, lanes]
            corrected[i, rows, lanes] = before + (0.75 * wide[near, k, rows] + 0.25 * wide[beside, k, rows])
    for i in range(6):
        rows = slice(16, 48) if i in (0, 5) else slice(8, 56)
        post[i, rows] = jacobi(corrected, i + 1, rows, dens[i + 1, rows.start - 8 : rows.stop - 8], 1.0)
    for i in range(4):
        out[i] = jacobi(post, i + 1, slice(16, 48), dens[i + 2, 8:40], 1.0)


def call(kernel, outs, scratch, *args):
    vmem = pl.BlockSpec(memory_space=pltpu.VMEM)
    shapes = [jax.ShapeDtypeStruct(shape, jnp.float32) for shape in outs]
    return pl.pallas_call(
        kernel,
        out_shape=shapes,
        in_specs=[vmem] * len(args),
        out_specs=[vmem] * len(outs),
        scratch_shapes=[pltpu.VMEM(shape, jnp.float32) for shape in scratch],
        compiler_params=pltpu.CompilerParams(vmem_limit_bytes=32 * 1024 * 1024),
    )(*args)


def send(values, axis, step):
    count = lax.axis_size(axis)
    return lax.ppermute(values, axis, [(i, (i + step) % count) for i in range(count)])


def rows_from_sides(near, far):
    last = [piece[:, 8:16] for piece in near]
    last += [jnp.concatenate([low[:, 12:16], high[:, 12:16]], 1) for low, high in far]
    first = [piece[:, 0:8] for piece in near]
    first += [jnp.concatenate([low[:, 0:4], high[:, 0:4]], 1) for low, high in far]
    return send(jnp.concatenate(last, 0), "gy", 1), send(jnp.concatenate(first, 0), "gy", -1)


def body(density, field):
    xlo = send(jnp.concatenate([field[1:4], density[2:4]], 0), "gx", 1)
    xhi = send(jnp.concatenate([field[0:3], density[0:2]], 0), "gx", -1)
    clo = send(jnp.concatenate([xlo[:, 28:32], xhi[:, 28:32], field[:, 28:32], density[:, 28:32]], 0), "gy", 1)
    chi = send(jnp.concatenate([xlo[:, 0:4], xhi[:, 0:4], field[:, 0:4], density[:, 0:4]], 0), "gy", -1)
    smooth, dens, own, own2, up, down = call(
        fine_kernel,
        [(6, 48, 256), (8, 48, 256), (4, 16, 128), (4, 16, 128), (4, 16, 128), (4, 16, 128)],
        [(10, 64, 256), (8, 64, 256), (4, 2, 32, 128), (64, 256)],
        field, density, xlo, xhi, clo, chi,
    )
    flo, fhi = send(own, "gx", 3), send(own2, "gx", -3)
    nlo = send(jnp.concatenate([flo[1:2], flo[3:4], own, fhi, up], 0), "gx", 1)
    nhi = send(jnp.concatenate([fhi[0:1], fhi[2:3], own, flo, down], 0), "gx", -1)
    yrows, zrows = rows_from_sides([own, nlo[2:10], nhi[2:10]], [(flo, fhi), (nlo[0:2], nhi[0:2])])
    (out,) = call(
        coarse_kernel,
        [(4, 32, 256)],
        [(16, 48, 128)] + [(16, 32, 128)] * 2 + [(16, 48, 128)] * 2 + [(6, 2, 64, 128), (8, 64, 256), (6, 64, 256)],
        smooth, dens, own, flo, fhi, nlo, nhi, zrows, yrows,
    )
    return out


def solution(mesh):
    placed = (P("gx", "gy", None), P("gx", "gy", None))
    return jax.shard_map(body, mesh=mesh, in_specs=placed, out_specs=P("gx", "gy", None), check_vma=False)
```

```python
import jax
import jax.numpy as jnp
from jax import lax
from jax.experimental import pallas as pl
from jax.experimental.pallas import tpu as pltpu
from jax.sharding import PartitionSpec as P

mass = 0.02
damping = 0.8


def pair_of(ref, i, start, rows):
    return ref[i, start - 1 : start - 1 + rows] + ref[i, start + 1 : start + 1 + rows]


def jacobi_rows(v, rows, below, above, source, inv_step):
    around = below + above + rows
    around = around + pltpu.roll(v, 1, 1) + pltpu.roll(v, v.shape[1] - 1, 1)
    square = v * v
    top = inv_step * around - source - v * ((6.0 * inv_step + mass) + (mass / 3.0) * square)
    return v + top / ((6.0 * inv_step + mass) / damping + (mass / damping) * square)


def jacobi(v, below, above, source, inv_step):
    around = below + above
    around = around + pltpu.roll(v, 1, 0) + pltpu.roll(v, v.shape[0] - 1, 0)
    around = around + pltpu.roll(v, 1, 1) + pltpu.roll(v, v.shape[1] - 1, 1)
    square = v * v
    top = inv_step * around - source - v * ((6.0 * inv_step + mass) + (mass / 3.0) * square)
    return v + top / ((6.0 * inv_step + mass) / damping + (mass / damping) * square)


def operator(v, below, above, inv_step):
    around = below + above
    around = around + pltpu.roll(v, 1, 0) + pltpu.roll(v, v.shape[0] - 1, 0)
    around = around + pltpu.roll(v, 1, 1) + pltpu.roll(v, v.shape[1] - 1, 1)
    return inv_step * around - v * ((6.0 * inv_step + mass) + (mass / 3.0) * (v * v))


def exact_dot(values, weights):
    high = values.astype(jnp.bfloat16)
    rest = values - high.astype(jnp.float32)
    middle = rest.astype(jnp.bfloat16)
    low = (rest - middle.astype(jnp.float32)).astype(jnp.bfloat16)
    total = jnp.dot(low, weights, preferred_element_type=jnp.float32)
    total = total + jnp.dot(middle, weights, preferred_element_type=jnp.float32)
    return total + jnp.dot(high, weights, preferred_element_type=jnp.float32)


def fine_kernel(field, density, xlo, xhi, chi, clo, smooth, dens, coarse, coarse2, up, down, f, d, s1, pair, rows):
    f[0:3, 8:40] = xlo[0:3]
    f[3:7, 8:40] = field[...]
    f[7:10, 8:40] = xhi[0:3]
    d[0:2, 8:40] = xlo[3:5]
    d[2:6, 8:40] = density[...]
    d[6:8, 8:40] = xhi[3:5]
    for side, at in ((clo, 4), (chi, 40)):
        f[0:3, at : at + 4] = side[0:3]
        f[3:7, at : at + 4] = side[10:14]
        f[7:10, at : at + 4] = side[5:8]
        d[0:2, at : at + 4] = side[3:5]
        d[2:6, at : at + 4] = side[14:18]
        d[6:8, at : at + 4] = side[8:10]
    for i in range(8):
        s1[i] = jacobi(f[i + 1], f[i], f[i + 2], d[i], 1.0)
    for i in range(6):
        smooth[i] = jacobi(s1[i + 1], s1[i], s1[i + 2], d[i + 1], 1.0)
    dens[...] = d[1:7]
    for j in range(2):
        total = smooth[2 * j + 1] + smooth[2 * j + 2]
        pair[j, 0], pair[j, 1] = total[:, 0:128], total[:, 128:256]
        defect = [
            d[i + 2] - operator(smooth[i + 1], smooth[i], smooth[i + 2], 1.0) for i in (2 * j, 2 * j + 1)
        ]
        total = defect[0] + defect[1]
        pair[j + 2, 0], pair[j + 2, 1] = total[:, 0:128], total[:, 128:256]
    for j in range(4):
        for k in range(2):
            total = pair[j, k, pl.ds(8, 16, stride=2)] + pair[j, k, pl.ds(9, 16, stride=2)]
            rows[16 * j : 16 * j + 16, 128 * k : 128 * k + 128] = total
    third = lax.broadcasted_iota(jnp.int32, (256, 128), 0)
    half = lax.broadcasted_iota(jnp.int32, (256, 128), 1)
    weights = jnp.where(third >> 1 == half, 0.125, 0.0).astype(jnp.bfloat16)
    coarse[...] = exact_dot(rows[...], weights).reshape(4, 16, 128)
    coarse2[...] = coarse[...]
    for face, layer in ((up, 3), (down, 2)):
        for j in range(4):
            at, lane = 8 + 16 * (j // 2), 128 * (j % 2)
            face[j] = smooth[layer, at : at + 16, lane : lane + 128]


def coarse_kernel(
    smooth, dens, own, flo, fhi, nlo, nhi, zrows, yrows,
    out, a, r, g, c0, c1, wide, corrected, post,
):
    for ref, at in ((a, 0), (r, 1)):
        ref[0:1, 8:24] = nlo[at : at + 1]
        ref[1:3, 8:24] = flo[2 * at : 2 * at + 2]
        ref[13:15, 8:24] = fhi[2 * at : 2 * at + 2]
        ref[15:16, 8:24] = nhi[at : at + 1]
        for rows, mine, low, high, start in (
            (slice(8, 24), own, nlo, nhi, 2),
            (slice(0, 8), yrows.at[0:4], yrows.at[4:12], yrows.at[12:20], 0),
            (slice(24, 32), zrows.at[0:4], zrows.at[4:12], zrows.at[12:20], 0),
        ):
            at_own, at_two = start + 2 * at, start + 4 + 2 * at
            ref[3:5, rows] = high[at_two : at_two + 2]
            ref[5:7, rows] = low[at_own : at_own + 2]
            ref[7:9, rows] = mine[2 * at : 2 * at + 2]
            ref[9:11, rows] = high[at_own : at_own + 2]
            ref[11:13, rows] = low[at_two : at_two + 2]
        for rows, side in ((slice(4, 8), yrows), (slice(24, 28), zrows)):
            ref[1:3, rows] = side[20 + 2 * at : 22 + 2 * at, 0:4]
            ref[0:1, rows] = side[24 + at : 25 + at, 0:4]
            ref[13:15, rows] = side[20 + 2 * at : 22 + 2 * at, 4:8]
            ref[15:16, rows] = side[24 + at : 25 + at, 4:8]
    for i in range(16):
        v = a[i]
        c0[i, 8:40] = v - r[i] / ((1.5 + mass) / damping + (mass / damping) * (v * v))
    for i in range(1, 15):
        g[i] = operator(a[i], a[i - 1], a[i + 1], 0.25) + r[i]
    now, later = c0, c1
    for sweep in range(1, 6):
        for i in range(sweep, 16 - sweep):
            later[i, 8:40] = jacobi_rows(now[i, 8:40], pair_of(now, i, 8, 32), now[i - 1, 8:40], now[i + 1, 8:40], g[i], 0.25)
        now, later = later, now
    change = (now[5:11, 8:40] - a[5:11]).reshape(192, 128)
    half = lax.broadcasted_iota(jnp.int32, (128, 256), 0)
    third = lax.broadcasted_iota(jnp.int32, (128, 256), 1)
    beside = ((third >> 1) + 2 * (third & 1) - 1) & 127
    weights = jnp.where(third >> 1 == half, 0.75, jnp.where(beside == half, 0.25, 0.0)).astype(jnp.bfloat16)
    spread = exact_dot(change, weights).reshape(6, 32, 256)
    for i in range(6):
        v = spread[i]
        even = 0.75 * v + 0.25 * pltpu.roll(v, 1, 0)
        odd = 0.75 * v + 0.25 * pltpu.roll(v, 31, 0)
        for k in range(2):
            wide[i, k, pl.ds(0, 32, stride=2)] = even[:, 128 * k : 128 * k + 128]
            wide[i, k, pl.ds(1, 32, stride=2)] = odd[:, 128 * k : 128 * k + 128]
    for j in range(4):
        at, lane = 8 + 16 * (j // 2), 128 * (j % 2)
        corrected[0, at : at + 16, lane : lane + 128] = nlo[10 + j]
        corrected[7, at : at + 16, lane : lane + 128] = nhi[10 + j]
    for i in range(8):
        near = i // 2 + 1
        beside_layer = near - 1 if i % 2 == 0 else near + 1
        before = corrected.at[i] if i in (0, 7) else smooth.at[i - 1]
        for k in range(2):
            lanes = slice(128 * k, 128 * k + 128)
            change = 0.75 * wide[near, k, 8:56] + 0.25 * wide[beside_layer, k, 8:56]
            corrected[i, :, lanes] = before[:, lanes] + change
    for i in range(6):
        post[i] = jacobi(corrected[i + 1], corrected[i], corrected[i + 2], dens[i], 1.0)
    for i in range(4):
        out[i] = jacobi(post[i + 1], post[i], post[i + 2], dens[i + 1], 1.0)[8:40]


def call(kernel, outs, scratch, *args):
    vmem = pl.BlockSpec(memory_space=pltpu.VMEM)
    shapes = [jax.ShapeDtypeStruct(shape, jnp.float32) for shape in outs]
    return pl.pallas_call(
        kernel,
        out_shape=shapes,
        in_specs=[vmem] * len(args),
        out_specs=[vmem] * len(outs),
        scratch_shapes=[pltpu.VMEM(shape, jnp.float32) for shape in scratch],
        compiler_params=pltpu.CompilerParams(vmem_limit_bytes=32 * 1024 * 1024),
    )(*args)


def send(values, axis, step):
    count = lax.axis_size(axis)
    return lax.ppermute(values, axis, [(i, (i + step) % count) for i in range(count)])


def rows_from_sides(near, far):
    last = [piece[:, 8:16] for piece in near]
    last += [jnp.concatenate([low[:, 12:16], high[:, 12:16]], 1) for low, high in far]
    first = [piece[:, 0:8] for piece in near]
    first += [jnp.concatenate([low[:, 0:4], high[:, 0:4]], 1) for low, high in far]
    return send(jnp.concatenate(last, 0), "gy", 1), send(jnp.concatenate(first, 0), "gy", -1)


def body(density, field):
    xlo = send(jnp.concatenate([field[1:4], density[2:4]], 0), "gx", 1)
    xhi = send(jnp.concatenate([field[0:3], density[0:2]], 0), "gx", -1)
    clo = send(jnp.concatenate([xlo[:, 28:32], xhi[:, 28:32], field[:, 28:32], density[:, 28:32]], 0), "gy", 1)
    chi = send(jnp.concatenate([xlo[:, 0:4], xhi[:, 0:4], field[:, 0:4], density[:, 0:4]], 0), "gy", -1)
    smooth, dens, own, own2, up, down = call(
        fine_kernel,
        [(6, 48, 256), (6, 48, 256), (4, 16, 128), (4, 16, 128), (4, 16, 128), (4, 16, 128)],
        [(10, 48, 256), (8, 48, 256), (8, 48, 256), (4, 2, 48, 128), (64, 256)],
        field, density, xlo, xhi, chi, clo,
    )
    flo, fhi = send(own, "gx", 3), send(own2, "gx", -3)
    nlo = send(jnp.concatenate([flo[1:2], flo[3:4], own, fhi, up], 0), "gx", 1)
    nhi = send(jnp.concatenate([fhi[0:1], fhi[2:3], own, flo, down], 0), "gx", -1)
    yrows, zrows = rows_from_sides([own, nlo[2:10], nhi[2:10]], [(flo, fhi), (nlo[0:2], nhi[0:2])])
    (out,) = call(
        coarse_kernel,
        [(4, 32, 256)],
        [(16, 32, 128)] * 3 + [(16, 48, 128)] * 2 + [(6, 2, 64, 128), (8, 48, 256), (6, 48, 256)],
        smooth, dens, own, flo, fhi, nlo, nhi, zrows, yrows,
    )
    return out


def solution(mesh):
    placed = (P("gx", "gy", None), P("gx", "gy", None))
    return jax.shard_map(body, mesh=mesh, in_specs=placed, out_specs=P("gx", "gy", None), check_vma=False)
```

```python
import jax
import jax.numpy as jnp
from jax import lax
from jax.experimental import pallas as pl
from jax.experimental.pallas import tpu as pltpu
from jax.sharding import PartitionSpec as P

mass = 0.02
damping = 0.8


def around(ref, i, rows):
    v, first, last = ref[i, rows], rows.start, rows.stop
    total = ref[i - 1, rows] + ref[i + 1, rows]
    total = total + (ref[i, first - 1 : last - 1] + ref[i, first + 1 : last + 1])
    return total + pltpu.roll(v, 1, 1) + pltpu.roll(v, v.shape[1] - 1, 1)


def jacobi(ref, i, rows, source, inv_step):
    v = ref[i, rows]
    square = v * v
    inner = (6.0 * inv_step + mass) + (mass / 3.0) * square
    top = inv_step * around(ref, i, rows) - source - v * inner
    return v + top / ((6.0 * inv_step + mass) / damping + (mass / damping) * square)


def operator(ref, i, rows, inv_step):
    v = ref[i, rows]
    return inv_step * around(ref, i, rows) - v * ((6.0 * inv_step + mass) + (mass / 3.0) * (v * v))


def exact_dot(values, weights):
    high = values.astype(jnp.bfloat16)
    rest = values - high.astype(jnp.float32)
    middle = rest.astype(jnp.bfloat16)
    low = (rest - middle.astype(jnp.float32)).astype(jnp.bfloat16)
    total = jnp.dot(low, weights, preferred_element_type=jnp.float32)
    total = total + jnp.dot(middle, weights, preferred_element_type=jnp.float32)
    return total + jnp.dot(high, weights, preferred_element_type=jnp.float32)


def fine_kernel(field, density, xlo, xhi, chi, clo, smooth, d, coarse, coarse2, up, down, f, s1, pair, rows):
    f[0:3, 16:48] = xlo[0:3]
    f[3:7, 16:48] = field[...]
    f[7:10, 16:48] = xhi[0:3]
    d[0:2, 8:40] = xlo[3:5]
    d[2:6, 8:40] = density[...]
    d[6:8, 8:40] = xhi[3:5]
    for side, at in ((clo, 4), (chi, 40)):
        f[0:3, at + 8 : at + 12] = side[0:3]
        f[3:7, at + 8 : at + 12] = side[10:14]
        f[7:10, at + 8 : at + 12] = side[5:8]
        d[0:2, at : at + 4] = side[3:5]
        d[2:6, at : at + 4] = side[14:18]
        d[6:8, at : at + 4] = side[8:10]
    for i in range(8):
        s1[i, 8:56] = jacobi(f, i + 1, slice(8, 56), d[i], 1.0)
    for i in range(6):
        smooth[i] = jacobi(s1, i + 1, slice(8, 56), d[i + 1], 1.0)
    for j in range(2):
        total = smooth[2 * j + 1, 8:40] + smooth[2 * j + 2, 8:40]
        pair[j, 0], pair[j, 1] = total[:, 0:128], total[:, 128:256]
        defect = [d[i + 2, 8:40] - operator(smooth, i + 1, slice(8, 40), 1.0) for i in (2 * j, 2 * j + 1)]
        total = defect[0] + defect[1]
        pair[j + 2, 0], pair[j + 2, 1] = total[:, 0:128], total[:, 128:256]
    for j in range(4):
        for k in range(2):
            total = pair[j, k, pl.ds(0, 16, stride=2)] + pair[j, k, pl.ds(1, 16, stride=2)]
            rows[16 * j : 16 * j + 16, 128 * k : 128 * k + 128] = total
    third = lax.broadcasted_iota(jnp.int32, (256, 128), 0)
    half = lax.broadcasted_iota(jnp.int32, (256, 128), 1)
    weights = jnp.where(third >> 1 == half, 0.125, 0.0).astype(jnp.bfloat16)
    coarse[...] = exact_dot(rows[...], weights).reshape(4, 16, 128)
    coarse2[...] = coarse[...]
    for face, layer in ((up, 3), (down, 2)):
        for j in range(4):
            at, lane = 8 + 16 * (j // 2), 128 * (j % 2)
            face[j] = smooth[layer, at : at + 16, lane : lane + 128]


def coarse_kernel(
    smooth, dens, own, flo, fhi, nlo, nhi, zrows, yrows,
    out, start, r, g, c0, c1, wide, corrected, post,
):
    for ref, at in ((start.at[:, 8:40], 0), (r, 1)):
        ref[0:1, 8:24] = nlo[at : at + 1]
        ref[1:3, 8:24] = flo[2 * at : 2 * at + 2]
        ref[13:15, 8:24] = fhi[2 * at : 2 * at + 2]
        ref[15:16, 8:24] = nhi[at : at + 1]
        for rows, mine, low, high, first in (
            (slice(8, 24), own, nlo, nhi, 2),
            (slice(0, 8), yrows.at[0:4], yrows.at[4:12], yrows.at[12:20], 0),
            (slice(24, 32), zrows.at[0:4], zrows.at[4:12], zrows.at[12:20], 0),
        ):
            at_own, at_two = first + 2 * at, first + 4 + 2 * at
            ref[3:5, rows] = high[at_two : at_two + 2]
            ref[5:7, rows] = low[at_own : at_own + 2]
            ref[7:9, rows] = mine[2 * at : 2 * at + 2]
            ref[9:11, rows] = high[at_own : at_own + 2]
            ref[11:13, rows] = low[at_two : at_two + 2]
        for rows, side in ((slice(4, 8), yrows), (slice(24, 28), zrows)):
            ref[1:3, rows] = side[20 + 2 * at : 22 + 2 * at, 0:4]
            ref[0:1, rows] = side[24 + at : 25 + at, 0:4]
            ref[13:15, rows] = side[20 + 2 * at : 22 + 2 * at, 4:8]
            ref[15:16, rows] = side[24 + at : 25 + at, 4:8]
    rows = slice(8, 40)
    for i in range(16):
        v = start[i, rows]
        c0[i, rows] = v - r[i] / ((1.5 + mass) / damping + (mass / damping) * (v * v))
    for i in range(1, 15):
        g[i] = operator(start, i, rows, 0.25) + r[i]
    now, later = c0, c1
    for sweep in range(1, 6):
        for i in range(sweep, 16 - sweep):
            later[i, rows] = jacobi(now, i, rows, g[i], 0.25)
        now, later = later, now
    change = (now[5:11, 8:40] - start[5:11, 8:40]).reshape(192, 128)
    half = lax.broadcasted_iota(jnp.int32, (128, 256), 0)
    third = lax.broadcasted_iota(jnp.int32, (128, 256), 1)
    beside = ((third >> 1) + 2 * (third & 1) - 1) & 127
    weights = jnp.where(third >> 1 == half, 0.75, jnp.where(beside == half, 0.25, 0.0)).astype(jnp.bfloat16)
    spread = exact_dot(change, weights).reshape(6, 32, 256)
    for i in range(6):
        v = spread[i]
        even = 0.75 * v + 0.25 * pltpu.roll(v, 1, 0)
        odd = 0.75 * v + 0.25 * pltpu.roll(v, 31, 0)
        for k in range(2):
            wide[i, k, pl.ds(0, 32, stride=2)] = even[:, 128 * k : 128 * k + 128]
            wide[i, k, pl.ds(1, 32, stride=2)] = odd[:, 128 * k : 128 * k + 128]
    for j in range(4):
        at, lane = 16 + 16 * (j // 2), 128 * (j % 2)
        corrected[0, at : at + 16, lane : lane + 128] = nlo[10 + j]
        corrected[7, at : at + 16, lane : lane + 128] = nhi[10 + j]
    for i in range(8):
        near = i // 2 + 1
        beside = near - 1 if i % 2 == 0 else near + 1
        for k in range(2):
            lanes = slice(128 * k, 128 * k + 128)
            if i in (0, 7):
                rows = slice(16, 48)
                before = corrected[i, rows, lanes]
            else:
                rows = slice(8, 56)
                before = smooth[i - 1, :, lanes]
            corrected[i, rows, lanes] = before + (0.75 * wide[near, k, rows] + 0.25 * wide[beside, k, rows])
    for i in range(6):
        rows = slice(16, 48) if i in (0, 5) else slice(8, 56)
        post[i, rows] = jacobi(corrected, i + 1, rows, dens[i + 1, rows.start - 8 : rows.stop - 8], 1.0)
    for i in range(4):
        out[i] = jacobi(post, i + 1, slice(16, 48), dens[i + 2, 8:40], 1.0)


def call(kernel, outs, scratch, *args):
    vmem = pl.BlockSpec(memory_space=pltpu.VMEM)
    shapes = [jax.ShapeDtypeStruct(shape, jnp.float32) for shape in outs]
    return pl.pallas_call(
        kernel,
        out_shape=shapes,
        in_specs=[vmem] * len(args),
        out_specs=[vmem] * len(outs),
        scratch_shapes=[pltpu.VMEM(shape, jnp.float32) for shape in scratch],
        compiler_params=pltpu.CompilerParams(vmem_limit_bytes=32 * 1024 * 1024),
    )(*args)


def send(values, axis, step):
    count = lax.axis_size(axis)
    return lax.ppermute(values, axis, [(i, (i + step) % count) for i in range(count)])


def rows_from_sides(near, far):
    last = [piece[:, 8:16] for piece in near]
    last += [jnp.concatenate([low[:, 12:16], high[:, 12:16]], 1) for low, high in far]
    first = [piece[:, 0:8] for piece in near]
    first += [jnp.concatenate([low[:, 0:4], high[:, 0:4]], 1) for low, high in far]
    return send(jnp.concatenate(last, 0), "gy", 1), send(jnp.concatenate(first, 0), "gy", -1)


def body(density, field):
    xlo = send(jnp.concatenate([field[1:4], density[2:4]], 0), "gx", 1)
    xhi = send(jnp.concatenate([field[0:3], density[0:2]], 0), "gx", -1)
    clo = send(jnp.concatenate([xlo[:, 28:32], xhi[:, 28:32], field[:, 28:32], density[:, 28:32]], 0), "gy", 1)
    chi = send(jnp.concatenate([xlo[:, 0:4], xhi[:, 0:4], field[:, 0:4], density[:, 0:4]], 0), "gy", -1)
    smooth, dens, own, own2, up, down = call(
        fine_kernel,
        [(6, 48, 256), (8, 48, 256), (4, 16, 128), (4, 16, 128), (4, 16, 128), (4, 16, 128)],
        [(10, 64, 256), (8, 64, 256), (4, 2, 32, 128), (64, 256)],
        field, density, xlo, xhi, chi, clo,
    )
    flo, fhi = send(own, "gx", 3), send(own2, "gx", -3)
    nlo = send(jnp.concatenate([flo[1:2], flo[3:4], own, fhi, up], 0), "gx", 1)
    nhi = send(jnp.concatenate([fhi[0:1], fhi[2:3], own, flo, down], 0), "gx", -1)
    yrows, zrows = rows_from_sides([own, nlo[2:10], nhi[2:10]], [(flo, fhi), (nlo[0:2], nhi[0:2])])
    (out,) = call(
        coarse_kernel,
        [(4, 32, 256)],
        [(16, 48, 128)] + [(16, 32, 128)] * 2 + [(16, 48, 128)] * 2 + [(6, 2, 64, 128), (8, 64, 256), (6, 64, 256)],
        smooth, dens, own, flo, fhi, nlo, nhi, zrows, yrows,
    )
    return out


def solution(mesh):
    placed = (P("gx", "gy", None), P("gx", "gy", None))
    return jax.shard_map(body, mesh=mesh, in_specs=placed, out_specs=P("gx", "gy", None), check_vma=False)
```

```python
import jax
import jax.numpy as jnp
from jax import lax
from jax.experimental import pallas as pl
from jax.experimental.pallas import tpu as pltpu
from jax.sharding import PartitionSpec as P

mass = 0.02
damping = 0.8


def around(ref, i, rows):
    v, first, last = ref[i, rows], rows.start, rows.stop
    total = ref[i - 1, rows] + ref[i + 1, rows]
    total = total + (ref[i, first - 1 : last - 1] + ref[i, first + 1 : last + 1])
    return total + pltpu.roll(v, 1, 1) + pltpu.roll(v, v.shape[1] - 1, 1)


def jacobi(ref, i, rows, source, inv_step):
    v = ref[i, rows]
    square = v * v
    inner = (6.0 * inv_step + mass) + (mass / 3.0) * square
    top = inv_step * around(ref, i, rows) - source - v * inner
    return v + top / ((6.0 * inv_step + mass) / damping + (mass / damping) * square)


def operator(ref, i, rows, inv_step):
    v = ref[i, rows]
    return inv_step * around(ref, i, rows) - v * ((6.0 * inv_step + mass) + (mass / 3.0) * (v * v))


def exact_dot(values, weights):
    high = values.astype(jnp.bfloat16)
    rest = values - high.astype(jnp.float32)
    middle = rest.astype(jnp.bfloat16)
    low = (rest - middle.astype(jnp.float32)).astype(jnp.bfloat16)
    total = jnp.dot(low, weights, preferred_element_type=jnp.float32)
    total = total + jnp.dot(middle, weights, preferred_element_type=jnp.float32)
    return total + jnp.dot(high, weights, preferred_element_type=jnp.float32)


def fine_kernel(field, density, xlo, xhi, chi, clo, smooth, d, coarse, coarse2, up, down, f, s1, pair, rows):
    f[0:3, 16:48] = xlo[0:3]
    f[3:7, 16:48] = field[...]
    f[7:10, 16:48] = xhi[0:3]
    d[0:2, 8:40] = xlo[3:5]
    d[2:6, 8:40] = density[...]
    d[6:8, 8:40] = xhi[3:5]
    for side, at, two in ((clo, 4, 6), (chi, 40, 40)):
        f[0:2, two + 8 : two + 10] = side[0:2, 2:4]
        f[8:10, two + 8 : two + 10] = side[0:2, 0:2]
        d[0:2, two : two + 2] = side[2:4, 2:4]
        d[6:8, two : two + 2] = side[2:4, 0:2]
        f[2, at + 8 : at + 12] = side[5]
        f[7, at + 8 : at + 12] = side[4]
        f[3:7, at + 8 : at + 12] = side[6:10]
        d[2:6, at : at + 4] = side[10:14]
    for i in range(8):
        s1[i, 8:56] = jacobi(f, i + 1, slice(8, 56), d[i], 1.0)
    for i in range(6):
        smooth[i] = jacobi(s1, i + 1, slice(8, 56), d[i + 1], 1.0)
    for j in range(2):
        total = smooth[2 * j + 1, 8:40] + smooth[2 * j + 2, 8:40]
        pair[j, 0], pair[j, 1] = total[:, 0:128], total[:, 128:256]
        defect = [d[i + 2, 8:40] - operator(smooth, i + 1, slice(8, 40), 1.0) for i in (2 * j, 2 * j + 1)]
        total = defect[0] + defect[1]
        pair[j + 2, 0], pair[j + 2, 1] = total[:, 0:128], total[:, 128:256]
    for j in range(4):
        for k in range(2):
            total = pair[j, k, pl.ds(0, 16, stride=2)] + pair[j, k, pl.ds(1, 16, stride=2)]
            rows[16 * j : 16 * j + 16, 128 * k : 128 * k + 128] = total
    third = lax.broadcasted_iota(jnp.int32, (256, 128), 0)
    half = lax.broadcasted_iota(jnp.int32, (256, 128), 1)
    weights = jnp.where(third >> 1 == half, 0.125, 0.0).astype(jnp.bfloat16)
    coarse[...] = exact_dot(rows[...], weights).reshape(4, 16, 128)
    coarse2[...] = coarse[...]
    for face, layer in ((up, 3), (down, 2)):
        for j in range(4):
            at, lane = 8 + 16 * (j // 2), 128 * (j % 2)
            face[j] = smooth[layer, at : at + 16, lane : lane + 128]


def coarse_kernel(
    smooth, dens, own, flo, fhi, nlo, nhi, zrows, yrows,
    out, start, r, g, c0, c1, wide, corrected, post,
):
    for ref, at in ((start.at[:, 8:40], 0), (r, 1)):
        ref[0:1, 8:24] = nlo[at : at + 1]
        ref[1:3, 8:24] = flo[2 * at : 2 * at + 2]
        ref[13:15, 8:24] = fhi[2 * at : 2 * at + 2]
        ref[15:16, 8:24] = nhi[at : at + 1]
        for rows, mine, low, high, first in (
            (slice(8, 24), own, nlo, nhi, 2),
            (slice(0, 8), yrows.at[0:4], yrows.at[4:12], yrows.at[12:20], 0),
            (slice(24, 32), zrows.at[0:4], zrows.at[4:12], zrows.at[12:20], 0),
        ):
            at_own, at_two = first + 2 * at, first + 4 + 2 * at
            ref[3:5, rows] = high[at_two : at_two + 2]
            ref[5:7, rows] = low[at_own : at_own + 2]
            ref[7:9, rows] = mine[2 * at : 2 * at + 2]
            ref[9:11, rows] = high[at_own : at_own + 2]
            ref[11:13, rows] = low[at_two : at_two + 2]
        for rows, side in ((slice(4, 8), yrows), (slice(24, 28), zrows)):
            ref[1:3, rows] = side[20 + 2 * at : 22 + 2 * at, 0:4]
            ref[0:1, rows] = side[24 + at : 25 + at, 0:4]
            ref[13:15, rows] = side[20 + 2 * at : 22 + 2 * at, 4:8]
            ref[15:16, rows] = side[24 + at : 25 + at, 4:8]
    rows = slice(8, 40)
    for i in range(16):
        v = start[i, rows]
        c0[i, rows] = v - r[i] / ((1.5 + mass) / damping + (mass / damping) * (v * v))
    for i in range(1, 15):
        g[i] = operator(start, i, rows, 0.25) + r[i]
    now, later = c0, c1
    for sweep in range(1, 6):
        for i in range(sweep, 16 - sweep):
            later[i, rows] = jacobi(now, i, rows, g[i], 0.25)
        now, later = later, now
    change = (now[5:11, 8:40] - start[5:11, 8:40]).reshape(192, 128)
    half = lax.broadcasted_iota(jnp.int32, (128, 256), 0)
    third = lax.broadcasted_iota(jnp.int32, (128, 256), 1)
    beside = ((third >> 1) + 2 * (third & 1) - 1) & 127
    weights = jnp.where(third >> 1 == half, 0.75, jnp.where(beside == half, 0.25, 0.0)).astype(jnp.bfloat16)
    spread = exact_dot(change, weights).reshape(6, 32, 256)
    for i in range(6):
        v = spread[i]
        even = 0.75 * v + 0.25 * pltpu.roll(v, 1, 0)
        odd = 0.75 * v + 0.25 * pltpu.roll(v, 31, 0)
        for k in range(2):
            wide[i, k, pl.ds(0, 32, stride=2)] = even[:, 128 * k : 128 * k + 128]
            wide[i, k, pl.ds(1, 32, stride=2)] = odd[:, 128 * k : 128 * k + 128]
    for j in range(4):
        at, lane = 16 + 16 * (j // 2), 128 * (j % 2)
        corrected[0, at : at + 16, lane : lane + 128] = nlo[10 + j]
        corrected[7, at : at + 16, lane : lane + 128] = nhi[10 + j]
    for i in range(8):
        near = i // 2 + 1
        beside = near - 1 if i % 2 == 0 else near + 1
        for k in range(2):
            lanes = slice(128 * k, 128 * k + 128)
            if i in (0, 7):
                rows = slice(16, 48)
                before = corrected[i, rows, lanes]
            else:
                rows = slice(8, 56)
                before = smooth[i - 1, :, lanes]
            corrected[i, rows, lanes] = before + (0.75 * wide[near, k, rows] + 0.25 * wide[beside, k, rows])
    for i in range(6):
        rows = slice(16, 48) if i in (0, 5) else slice(8, 56)
        post[i, rows] = jacobi(corrected, i + 1, rows, dens[i + 1, rows.start - 8 : rows.stop - 8], 1.0)
    for i in range(4):
        out[i] = jacobi(post, i + 1, slice(16, 48), dens[i + 2, 8:40], 1.0)


def call(kernel, outs, scratch, *args):
    vmem = pl.BlockSpec(memory_space=pltpu.VMEM)
    shapes = [jax.ShapeDtypeStruct(shape, jnp.float32) for shape in outs]
    return pl.pallas_call(
        kernel,
        out_shape=shapes,
        in_specs=[vmem] * len(args),
        out_specs=[vmem] * len(outs),
        scratch_shapes=[pltpu.VMEM(shape, jnp.float32) for shape in scratch],
        compiler_params=pltpu.CompilerParams(vmem_limit_bytes=32 * 1024 * 1024),
    )(*args)


def send(values, axis, step):
    count = lax.axis_size(axis)
    return lax.ppermute(values, axis, [(i, (i + step) % count) for i in range(count)])


def edge_rows(field, density, xlo, xhi, four, two):
    outer = [jnp.concatenate([xhi[j, two], xlo[i, two]], 1) for i, j in ((slice(0, 2), slice(1, 3)), (slice(3, 5), slice(3, 5)))]
    return jnp.concatenate(outer + [xhi[0:1, four], xlo[2:3, four], field[:, four], density[:, four]], 0)


def rows_from_sides(near, far):
    last = [piece[:, 8:16] for piece in near]
    last += [jnp.concatenate([low[:, 12:16], high[:, 12:16]], 1) for low, high in far]
    first = [piece[:, 0:8] for piece in near]
    first += [jnp.concatenate([low[:, 0:4], high[:, 0:4]], 1) for low, high in far]
    return send(jnp.concatenate(last, 0), "gy", 1), send(jnp.concatenate(first, 0), "gy", -1)


def body(density, field):
    xlo = send(jnp.concatenate([field[1:4], density[2:4]], 0), "gx", 1)
    xhi = send(jnp.concatenate([field[0:3], density[0:2]], 0), "gx", -1)
    clo = send(edge_rows(field, density, xlo, xhi, slice(28, 32), slice(30, 32)), "gy", 1)
    chi = send(edge_rows(field, density, xlo, xhi, slice(0, 4), slice(0, 2)), "gy", -1)
    smooth, dens, own, own2, up, down = call(
        fine_kernel,
        [(6, 48, 256), (8, 48, 256), (4, 16, 128), (4, 16, 128), (4, 16, 128), (4, 16, 128)],
        [(10, 64, 256), (8, 64, 256), (4, 2, 32, 128), (64, 256)],
        field, density, xlo, xhi, chi, clo,
    )
    flo, fhi = send(own, "gx", 3), send(own2, "gx", -3)
    nlo = send(jnp.concatenate([flo[1:2], flo[3:4], own, fhi, up], 0), "gx", 1)
    nhi = send(jnp.concatenate([fhi[0:1], fhi[2:3], own, flo, down], 0), "gx", -1)
    yrows, zrows = rows_from_sides([own, nlo[2:10], nhi[2:10]], [(flo, fhi), (nlo[0:2], nhi[0:2])])
    (out,) = call(
        coarse_kernel,
        [(4, 32, 256)],
        [(16, 48, 128)] + [(16, 32, 128)] * 2 + [(16, 48, 128)] * 2 + [(6, 2, 64, 128), (8, 64, 256), (6, 64, 256)],
        smooth, dens, own, flo, fhi, nlo, nhi, zrows, yrows,
    )
    return out


def solution(mesh):
    placed = (P("gx", "gy", None), P("gx", "gy", None))
    return jax.shard_map(body, mesh=mesh, in_specs=placed, out_specs=P("gx", "gy", None), check_vma=False)
```

```python
import jax
import jax.numpy as jnp
from jax import lax
from jax.experimental import pallas as pl
from jax.experimental.pallas import tpu as pltpu
from jax.sharding import PartitionSpec as P

mass = 0.02
damping = 0.8


def around(ref, i, rows):
    v, first, last = ref[i, rows], rows.start, rows.stop
    total = ref[i - 1, rows] + ref[i + 1, rows]
    total = total + (ref[i, first - 1 : last - 1] + ref[i, first + 1 : last + 1])
    return total + pltpu.roll(v, 1, 1) + pltpu.roll(v, v.shape[1] - 1, 1)


def jacobi(ref, i, rows, source, area):
    v = ref[i, rows]
    square = v * v
    top = around(ref, i, rows) - source - v * ((6.0 + area * mass) + (area * mass / 3.0) * square)
    return v + top / ((6.0 + area * mass) / damping + (area * mass / damping) * square)


def operator(ref, i, rows, area):
    v = ref[i, rows]
    return around(ref, i, rows) - v * ((6.0 + area * mass) + (area * mass / 3.0) * (v * v))


def exact_dot(values, weights):
    high = values.astype(jnp.bfloat16)
    rest = values - high.astype(jnp.float32)
    middle = rest.astype(jnp.bfloat16)
    low = (rest - middle.astype(jnp.float32)).astype(jnp.bfloat16)
    total = jnp.dot(low, weights, preferred_element_type=jnp.float32)
    total = total + jnp.dot(middle, weights, preferred_element_type=jnp.float32)
    return total + jnp.dot(high, weights, preferred_element_type=jnp.float32)


def fine_kernel(field, density, xlo, xhi, chi, clo, smooth, d, coarse, coarse2, up, down, f, s1, pair, rows):
    f[0:3, 16:48] = xlo[0:3]
    f[3:7, 16:48] = field[...]
    f[7:10, 16:48] = xhi[0:3]
    d[0:2, 8:40] = xlo[3:5]
    d[2:6, 8:40] = density[...]
    d[6:8, 8:40] = xhi[3:5]
    for side, at, two in ((clo, 4, 6), (chi, 40, 40)):
        f[0:2, two + 8 : two + 10] = side[0:2, 2:4]
        f[8:10, two + 8 : two + 10] = side[0:2, 0:2]
        d[0:2, two : two + 2] = side[2:4, 2:4]
        d[6:8, two : two + 2] = side[2:4, 0:2]
        f[2, at + 8 : at + 12] = side[5]
        f[7, at + 8 : at + 12] = side[4]
        f[3:7, at + 8 : at + 12] = side[6:10]
        d[2:6, at : at + 4] = side[10:14]
    for i in range(8):
        s1[i, 8:56] = jacobi(f, i + 1, slice(8, 56), d[i], 1.0)
    for i in range(6):
        smooth[i] = jacobi(s1, i + 1, slice(8, 56), d[i + 1], 1.0)
    for j in range(2):
        total = smooth[2 * j + 1, 8:40] + smooth[2 * j + 2, 8:40]
        pair[j, 0], pair[j, 1] = total[:, 0:128], total[:, 128:256]
        defect = [d[i + 2, 8:40] - operator(smooth, i + 1, slice(8, 40), 1.0) for i in (2 * j, 2 * j + 1)]
        total = defect[0] + defect[1]
        pair[j + 2, 0], pair[j + 2, 1] = total[:, 0:128], total[:, 128:256]
    for j in range(4):
        for k in range(2):
            total = pair[j, k, pl.ds(0, 16, stride=2)] + pair[j, k, pl.ds(1, 16, stride=2)]
            rows[16 * j : 16 * j + 16, 128 * k : 128 * k + 128] = total
    third = lax.broadcasted_iota(jnp.int32, (256, 128), 0)
    half = lax.broadcasted_iota(jnp.int32, (256, 128), 1)
    weights = jnp.where(third >> 1 == half, 0.125, 0.0).astype(jnp.bfloat16)
    coarse[...] = exact_dot(rows[...], weights).reshape(4, 16, 128)
    coarse2[...] = coarse[...]
    for face, layer in ((up, 3), (down, 2)):
        for j in range(4):
            at, lane = 8 + 16 * (j // 2), 128 * (j % 2)
            face[j] = smooth[layer, at : at + 16, lane : lane + 128]


def coarse_kernel(
    smooth, dens, own, flo, fhi, nlo, nhi, zrows, yrows,
    out, start, r, g, c0, c1, wide, corrected, post,
):
    for ref, at in ((start.at[:, 8:40], 0), (r, 1)):
        ref[0:1, 8:24] = nlo[at : at + 1]
        ref[1:3, 8:24] = flo[2 * at : 2 * at + 2]
        ref[13:15, 8:24] = fhi[2 * at : 2 * at + 2]
        ref[15:16, 8:24] = nhi[at : at + 1]
        for rows, mine, low, high, first in (
            (slice(8, 24), own, nlo, nhi, 2),
            (slice(0, 8), yrows.at[0:4], yrows.at[4:12], yrows.at[12:20], 0),
            (slice(24, 32), zrows.at[0:4], zrows.at[4:12], zrows.at[12:20], 0),
        ):
            at_own, at_two = first + 2 * at, first + 4 + 2 * at
            ref[3:5, rows] = high[at_two : at_two + 2]
            ref[5:7, rows] = low[at_own : at_own + 2]
            ref[7:9, rows] = mine[2 * at : 2 * at + 2]
            ref[9:11, rows] = high[at_own : at_own + 2]
            ref[11:13, rows] = low[at_two : at_two + 2]
        for rows, side in ((slice(4, 8), yrows), (slice(24, 28), zrows)):
            ref[1:3, rows] = side[20 + 2 * at : 22 + 2 * at, 0:4]
            ref[0:1, rows] = side[24 + at : 25 + at, 0:4]
            ref[13:15, rows] = side[20 + 2 * at : 22 + 2 * at, 4:8]
            ref[15:16, rows] = side[24 + at : 25 + at, 4:8]
    rows = slice(8, 40)
    for i in range(16):
        v = start[i, rows]
        c0[i, rows] = v - r[i] / ((1.5 + mass) / damping + (mass / damping) * (v * v))
    for i in range(1, 15):
        g[i] = operator(start, i, rows, 4.0) + 4.0 * r[i]
    now, later = c0, c1
    for sweep in range(1, 6):
        for i in range(sweep, 16 - sweep):
            later[i, rows] = jacobi(now, i, rows, g[i], 4.0)
        now, later = later, now
    change = (now[5:11, 8:40] - start[5:11, 8:40]).reshape(192, 128)
    half = lax.broadcasted_iota(jnp.int32, (128, 256), 0)
    third = lax.broadcasted_iota(jnp.int32, (128, 256), 1)
    beside = ((third >> 1) + 2 * (third & 1) - 1) & 127
    weights = jnp.where(third >> 1 == half, 0.75, jnp.where(beside == half, 0.25, 0.0)).astype(jnp.bfloat16)
    spread = exact_dot(change, weights).reshape(6, 32, 256)
    for i in range(6):
        v = spread[i]
        even = 0.75 * v + 0.25 * pltpu.roll(v, 1, 0)
        odd = 0.75 * v + 0.25 * pltpu.roll(v, 31, 0)
        for k in range(2):
            wide[i, k, pl.ds(0, 32, stride=2)] = even[:, 128 * k : 128 * k + 128]
            wide[i, k, pl.ds(1, 32, stride=2)] = odd[:, 128 * k : 128 * k + 128]
    for j in range(4):
        at, lane = 16 + 16 * (j // 2), 128 * (j % 2)
        corrected[0, at : at + 16, lane : lane + 128] = nlo[10 + j]
        corrected[7, at : at + 16, lane : lane + 128] = nhi[10 + j]
    for i in range(8):
        near = i // 2 + 1
        beside = near - 1 if i % 2 == 0 else near + 1
        for k in range(2):
            lanes = slice(128 * k, 128 * k + 128)
            if i in (0, 7):
                rows = slice(16, 48)
                before = corrected[i, rows, lanes]
            else:
                rows = slice(8, 56)
                before = smooth[i - 1, :, lanes]
            corrected[i, rows, lanes] = before + (0.75 * wide[near, k, rows] + 0.25 * wide[beside, k, rows])
    for i in range(6):
        rows = slice(16, 48) if i in (0, 5) else slice(8, 56)
        post[i, rows] = jacobi(corrected, i + 1, rows, dens[i + 1, rows.start - 8 : rows.stop - 8], 1.0)
    for i in range(4):
        out[i] = jacobi(post, i + 1, slice(16, 48), dens[i + 2, 8:40], 1.0)


def call(kernel, outs, scratch, *args):
    vmem = pl.BlockSpec(memory_space=pltpu.VMEM)
    shapes = [jax.ShapeDtypeStruct(shape, jnp.float32) for shape in outs]
    return pl.pallas_call(
        kernel,
        out_shape=shapes,
        in_specs=[vmem] * len(args),
        out_specs=[vmem] * len(outs),
        scratch_shapes=[pltpu.VMEM(shape, jnp.float32) for shape in scratch],
        compiler_params=pltpu.CompilerParams(vmem_limit_bytes=32 * 1024 * 1024),
    )(*args)


def send(values, axis, step):
    count = lax.axis_size(axis)
    return lax.ppermute(values, axis, [(i, (i + step) % count) for i in range(count)])


def edge_rows(field, density, xlo, xhi, four, two):
    outer = [jnp.concatenate([xhi[j, two], xlo[i, two]], 1) for i, j in ((slice(0, 2), slice(1, 3)), (slice(3, 5), slice(3, 5)))]
    return jnp.concatenate(outer + [xhi[0:1, four], xlo[2:3, four], field[:, four], density[:, four]], 0)


def rows_from_sides(near, far):
    last = [piece[:, 8:16] for piece in near]
    last += [jnp.concatenate([low[:, 12:16], high[:, 12:16]], 1) for low, high in far]
    first = [piece[:, 0:8] for piece in near]
    first += [jnp.concatenate([low[:, 0:4], high[:, 0:4]], 1) for low, high in far]
    return send(jnp.concatenate(last, 0), "gy", 1), send(jnp.concatenate(first, 0), "gy", -1)


def body(density, field):
    xlo = send(jnp.concatenate([field[1:4], density[2:4]], 0), "gx", 1)
    xhi = send(jnp.concatenate([field[0:3], density[0:2]], 0), "gx", -1)
    clo = send(edge_rows(field, density, xlo, xhi, slice(28, 32), slice(30, 32)), "gy", 1)
    chi = send(edge_rows(field, density, xlo, xhi, slice(0, 4), slice(0, 2)), "gy", -1)
    smooth, dens, own, own2, up, down = call(
        fine_kernel,
        [(6, 48, 256), (8, 48, 256), (4, 16, 128), (4, 16, 128), (4, 16, 128), (4, 16, 128)],
        [(10, 64, 256), (8, 64, 256), (4, 2, 32, 128), (64, 256)],
        field, density, xlo, xhi, chi, clo,
    )
    flo, fhi = send(own, "gx", 3), send(own2, "gx", -3)
    nlo = send(jnp.concatenate([flo[1:2], flo[3:4], own, fhi, up], 0), "gx", 1)
    nhi = send(jnp.concatenate([fhi[0:1], fhi[2:3], own, flo, down], 0), "gx", -1)
    yrows, zrows = rows_from_sides([own, nlo[2:10], nhi[2:10]], [(flo, fhi), (nlo[0:2], nhi[0:2])])
    (out,) = call(
        coarse_kernel,
        [(4, 32, 256)],
        [(16, 48, 128)] + [(16, 32, 128)] * 2 + [(16, 48, 128)] * 2 + [(6, 2, 64, 128), (8, 64, 256), (6, 64, 256)],
        smooth, dens, own, flo, fhi, nlo, nhi, zrows, yrows,
    )
    return out


def solution(mesh):
    placed = (P("gx", "gy", None), P("gx", "gy", None))
    return jax.shard_map(body, mesh=mesh, in_specs=placed, out_specs=P("gx", "gy", None), check_vma=False)
```
